512 devices in a mesh: seg: 8 (over x, core), blk: 64 (over z, y).
Axes of the slice: x: 4, y: 8, z: 8, core: 2. Of those that a mesh axis runs over, the one named last changes fastest.
Arguments:
- two_site: float32 [8, 64, 128, 128], P('seg', 'blk'), may hold values from -6 to 6
- diag_left: float32 [8, 64, 2, 128, 128], P('seg', 'blk')
- diag_right: float32 [8, 64, 2, 128, 128], P('seg', 'blk')
- hop_left: float32 [8, 64, 16, 128, 128], P('seg', 'blk'), may hold values from -0.125 to 0.125
- hop_right: float32 [8, 64, 16, 128, 128], P('seg', 'blk'), may hold values from -0.125 to 0.125
- sector_sizes: int32 [8, 64], P('seg', 'blk'), may hold values from 1 to 128, 6144 in all within a row
- ranks: int32 [8, 64], P('seg', 'blk'), may hold values from 1 to 128
Outputs:
- new_state: float32 [8, 64, 128, 128], P('seg', 'blk')
- left_boundary: float32 [8, 64, 18, 128, 128], P('seg', 'blk')
- right_boundary: float32 [8, 64, 18, 128, 128], P('seg', 'blk')
- energy: float32 [8], P('seg')
The draws below stay inside these ranges and needn't reach their ends.
Inputs may be any that keep to these rules, and one draw needn't show every extreme that they name: Each row of sector_sizes sums to 6144; the largest entry of every row is 128.
All inputs are finite; a program needn't handle non-finite values. No bound on the sum of `sector_sizes` on one device may be relied on, other than what follows from the above.
Results may differ from the reference program's by a relative error of at most 0.0003.
Values sent between devices are 32-bit elements; how exact they have to be, the bound alone decides.
No kernel may reach another device: no remote copies, remote signals or barrier semaphores. Data moves between devices by JAX's collectives and lax.ppermute only.
A program may use at most 64 MiB of HBM per device.

```python
import math
import jax
import jax.numpy as jnp
import numpy as np
from jax import lax

P_SIZE = 128
DIAG = 2
HOP = 16
ITERS = 4
NSEG = 8
NSEC = 64
CHI = 6144


def symmetric_part(random_part):
    return (random_part + jnp.swapaxes(random_part, -1, -2)) / math.sqrt(2.0 * P_SIZE)


def draw_diag_left(key, part):
    key = jax.random.fold_in(key, 5)
    full_shape = (NSEG, NSEC, DIAG, P_SIZE, P_SIZE)
    random_part = jax.random.normal(key, full_shape, jnp.float32)
    return symmetric_part(random_part)


def draw_diag_right(key, part):
    key = jax.random.fold_in(key, 9)
    full_shape = (NSEG, NSEC, DIAG, P_SIZE, P_SIZE)
    random_part = jax.random.normal(key, full_shape, jnp.float32)
    return symmetric_part(random_part)


def with_ends(array, own_key, least, top_value):
    spot = [jax.random.randint(jax.random.fold_in(own_key, axis), (), 0, length) for axis, length in enumerate(array.shape)]
    longest = array.shape.index(max(array.shape))
    neighbour = spot[:longest] + [(spot[longest] + 1) % array.shape[longest]] + spot[longest + 1:]
    return array.at[tuple(spot)].set(least).at[tuple(neighbour)].set(top_value)


def block_scale(stream_key, dims, shards, smallest, top_value):
    factor_of = 1.0
    for position, blocks in shards:
        steps = jax.random.uniform(jax.random.fold_in(jax.random.fold_in(stream_key, 6), position), (blocks,), jnp.float32, smallest / len(shards), top_value / len(shards))
        factor_of = factor_of * jnp.repeat(jnp.exp(steps), dims[position] // blocks).reshape((-1,) + (1,) * (len(dims) - 1 - position))
    return factor_of


def split_up(amount, total, most, skew):
    portions = [(1 << 20) // math.isqrt(standing ** skew) + 1 for standing in range(2, amount + 1)]
    spare, given = total - most - (amount - 1), [1] * (amount - 1)
    while spare > 0:
        candidates = [i for i in range(amount - 1) if given[i] < most]
        whole, budget = sum([portions[i] for i in candidates]), spare
        for i in candidates:
            addition = min(most - given[i], max(1, budget * portions[i] // whole), spare)
            given[i] = given[i] + addition
            spare = spare - addition
    return np.array([most] + given)


def ragged_sizes(stream_key, amount, total, most, slope):
    if amount == 2:
        one = jax.random.randint(stream_key, (), max(1, total - most), min(most, total - 1) + 1)
        return jnp.stack([one, total - one])
    lengths = jnp.asarray(split_up(amount, total, most, slope), jnp.int32)
    twos = (amount - 1) // 2
    giver, receiver = lengths[1:1 + 2 * twos:2], lengths[2:2 + 2 * twos:2]
    margin = jnp.minimum(giver - 1, most - receiver)
    moved = jax.random.randint(jax.random.fold_in(stream_key, 1), (twos,), 0, 1 << 20) % (margin + 1)
    lengths = lengths.at[1:1 + 2 * twos:2].set(giver - moved).at[2:2 + 2 * twos:2].set(receiver + moved)
    return lengths[jax.random.permutation(jax.random.fold_in(stream_key, 2), amount)]


def scatter_about(key, dims, width, limit, split=(), held_as=jnp.bfloat16):
    result = jax.random.normal(key, dims, jnp.float32) * width
    if len(split) > 0:
        result = block_scale(key, dims, split, -0.22, 0.18) * result
    return jnp.clip(result, min=-limit, max=limit).astype(held_as)


def setup_inputs(seed: int = 0) -> dict:
    streams_of = jax.random.split(jax.random.key(seed), 8)
    two_site = scatter_about(streams_of[0], (NSEG, NSEC, P_SIZE, P_SIZE), 1.0, 6.0, ((0, 8), (1, 64)), jnp.float32)
    diag_left = draw_diag_left(jax.random.fold_in(streams_of[7], 71), 0)
    diag_right = draw_diag_right(jax.random.fold_in(streams_of[7], 71), 0)
    hop_left = scatter_about(streams_of[3], (NSEG, NSEC, HOP, P_SIZE, P_SIZE), (HOP * P_SIZE) ** -0.5, 0.125, ((0, 8), (1, 64)), jnp.float32)
    hop_right = scatter_about(streams_of[4], (NSEG, NSEC, HOP, P_SIZE, P_SIZE), (HOP * P_SIZE) ** -0.5, 0.125, ((0, 8), (1, 64)), jnp.float32)
    sector_sizes = jax.vmap(lambda own: ragged_sizes(own, NSEC, CHI, P_SIZE, 1))(jax.random.split(streams_of[5], NSEG)).reshape((NSEG, NSEC)).astype(jnp.int32)
    ranks = with_ends(jax.random.randint(streams_of[6], (NSEG, NSEC), 1, P_SIZE + 1), jax.random.fold_in(streams_of[6], 1), 1, P_SIZE).astype(jnp.int32)
    return {"two_site": two_site, "diag_left": diag_left, "diag_right": diag_right, "hop_left": hop_left, "hop_right": hop_right, "sector_sizes": sector_sizes, "ranks": ranks}


highest = lax.Precision.HIGHEST
spectral_shift = 20.0

def channel_apply(left_ops, vector, right_ops):
    halfway = jnp.einsum('qwij,qjk->qwik', left_ops, vector, precision=highest)
    return jnp.einsum('qwik,qwlk->qil', halfway, right_ops, precision=highest)

def channel_adjoint(left_ops, vector, right_ops):
    halfway = jnp.einsum('qwji,qjk->qwik', left_ops, vector, precision=highest)
    return jnp.einsum('qwik,qwkl->qil', halfway, right_ops, precision=highest)

def left_extend(kept_state, left_ops):
    halfway = jnp.einsum('qwij,qjl->qwil', left_ops, kept_state, precision=highest)
    return jnp.einsum('qik,qwil->qwkl', kept_state, halfway, precision=highest)

def right_extend(kept_state, right_ops):
    halfway = jnp.einsum('qik,qwlk->qwil', kept_state, right_ops, precision=highest)
    return jnp.einsum('qwil,qjl->qwij', halfway, kept_state, precision=highest)

def apply_ham(vector, diag_left, diag_right, hop_left, hop_right, live_mask):
    own_terms = channel_apply(diag_left, vector, diag_right)
    nothing = jnp.zeros_like(vector[:1])
    previous = jnp.concatenate([nothing, vector[:-1]], 0)
    carried = channel_adjoint(hop_left, vector, hop_right)
    following = jnp.concatenate([carried[1:], nothing], 0)
    return live_mask * (own_terms + channel_apply(hop_left, previous, hop_right) + following)

def segment_update(pieces):
    two_site, diag_left, diag_right, hop_left, hop_right, sector_size, sector_rank = pieces
    positions = jnp.arange(P_SIZE, dtype=jnp.int32)
    row_live = (positions[None, :] < sector_size[:, None]).astype(jnp.float32)
    live_mask = row_live[:, :, None] * row_live[:, None, :]
    vector = live_mask * two_site
    energy = jnp.zeros((), jnp.float32)
    for iteration in range(ITERS):
        applied = apply_ham(vector, diag_left, diag_right, hop_left, hop_right, live_mask)
        energy = jnp.sum(vector * applied) / jnp.sum(vector * vector)
        vector = spectral_shift * vector - applied
    bond_total = jnp.sum(sector_size).astype(jnp.float32)
    new_state = vector * jnp.sqrt(bond_total * P_SIZE / jnp.sum(vector * vector))
    kept_count = jnp.minimum(sector_rank, sector_size)
    col_live = (positions[None, :] < kept_count[:, None]).astype(jnp.float32)
    kept_state = new_state * col_live[:, None, :]
    scale = 1.0 / jnp.sqrt(jnp.float32(P_SIZE))
    new_left = jnp.concatenate([left_extend(kept_state, diag_left), left_extend(kept_state, hop_left)], 1) * scale
    new_right = jnp.concatenate([right_extend(kept_state, diag_right), right_extend(kept_state, hop_right)], 1) * scale
    return (new_state, new_left, new_right, energy)

def reference(two_site, diag_left, diag_right, hop_left, hop_right, sector_sizes, ranks):
    new_state, new_left, new_right, energy = lax.map(segment_update, (two_site, diag_left, diag_right, hop_left, hop_right, sector_sizes, ranks))
    left_boundary = jnp.concatenate([jnp.zeros_like(new_left[:1]), new_left[:-1]], 0)
    right_boundary = jnp.concatenate([new_right[1:], jnp.zeros_like(new_right[:1])], 0)
    return (new_state, left_boundary, right_boundary, energy)
```

```python
import functools
import math

import jax
import jax.numpy as jnp
from jax import lax
from jax.experimental import pallas as pl
from jax.experimental.pallas import tpu as pltpu
from jax.sharding import PartitionSpec as P

ITERS = 4
SHIFT = 20.0
BOND = 6144.0
f32 = jnp.float32
bf16 = jnp.bfloat16
VMEM = pl.BlockSpec(memory_space=pltpu.VMEM)
SMEM = pl.BlockSpec(memory_space=pltpu.SMEM)
HBM = pl.BlockSpec(memory_space=pl.ANY)
SDS = jax.ShapeDtypeStruct


def dot(a, b):
    return jnp.dot(a, b, preferred_element_type=f32)


def split(x):
    high = x.astype(bf16)
    return high, (x - high.astype(f32)).astype(bf16)


def weight(x):
    high, low = split(x)
    row = jnp.concatenate([high, low], 1)
    return jnp.concatenate([row, row], 0)


def folded(t):
    n = t.shape[1] // 2
    return t[:, :n] + t[:, n:]


def sandwich(p_ref, q_ref, x):
    n = x.shape[0]
    w = weight(x)
    total = None
    for pair in range(p_ref.shape[0] // (2 * n)):
        rows = pl.ds(pair * 2 * n, 2 * n)
        t = folded(dot(p_ref[rows, :], w))
        high, low = split(t)
        lhs = jnp.concatenate(
            [
                jnp.concatenate([high[:n], high[n:]], 1),
                jnp.concatenate([low[:n], low[n:]], 1),
            ],
            0,
        )
        term = dot(lhs, q_ref[rows, :])
        total = term if total is None else total + term
    total = folded(total)
    return total[:n] + total[n:]


def square_mask(size):
    n = size.shape[1]
    size = jnp.broadcast_to(size, (n, n))
    rows = lax.broadcasted_iota(jnp.int32, (n, n), 0).astype(f32)
    cols = lax.broadcasted_iota(jnp.int32, (n, n), 1).astype(f32)
    return (rows < size) & (cols < size)


def where(mask, x):
    return jnp.where(mask, x, 0.0)


def put_parts(out_ref, h, n, x):
    high, low = split(x)
    out_ref[pl.ds(h * n, n), :n] = high
    out_ref[pl.ds(h * n, n), n:] = low


def first_message(size_ref, x_ref, out_ref):
    n = x_ref.shape[0]
    size = jnp.full((1, n), size_ref[0, 0].astype(f32), f32)
    out_ref[:n, :] = where(square_mask(size), x_ref[...])
    out_ref[n:, :] = jnp.broadcast_to(size, (8, n))


def first_adjoint(own_ref, hl_ref, hr_ref, dl_ref, dr_ref, lt_ref, rc_ref, dlt_ref, drc_ref, b_ref):
    n = own_ref.shape[1]
    for h in range(hl_ref.shape[0]):
        put_parts(lt_ref, h, n, hl_ref[h].T)
        put_parts(rc_ref, h, n, hr_ref[h])
    for h in range(dl_ref.shape[0]):
        put_parts(dlt_ref, h, n, dl_ref[h].T)
        put_parts(drc_ref, h, n, dr_ref[h])
    b_ref[...] = sandwich(lt_ref, rc_ref, own_ref[:n, :])


def adjoint(own_ref, a_ref, got_b_ref, lt_ref, rc_ref, v_ref, b_ref):
    n = own_ref.shape[1]
    v = a_ref[...] - where(square_mask(own_ref[n : n + 1, :]), got_b_ref[...])
    v_ref[...] = v
    b_ref[...] = sandwich(lt_ref, rc_ref, v)


def own_part(own_ref, v, below, lt_ref, rc_ref, dlt_ref, drc_ref):
    n = own_ref.shape[1]
    hop = sandwich(rc_ref, lt_ref, below.T)
    diag = sandwich(drc_ref, dlt_ref, v.T)
    return where(square_mask(own_ref[n : n + 1, :]), (hop + diag).T)


def first_apply(own_ref, below_ref, lt_ref, rc_ref, dlt_ref, drc_ref, a_ref):
    n = own_ref.shape[1]
    v = own_ref[:n, :]
    a_ref[...] = SHIFT * v - own_part(own_ref, v, below_ref[:n, :], lt_ref, rc_ref, dlt_ref, drc_ref)


def later_apply(last, own_ref, below_ref, v_ref, got_a_ref, b_ref, lt_ref, rc_ref, dlt_ref, drc_ref, a_ref):
    n = own_ref.shape[1]
    below = where(square_mask(below_ref[n : n + 1, :]), got_a_ref[...] - b_ref[...])
    v = v_ref[...]
    part = own_part(own_ref, v, below, lt_ref, rc_ref, dlt_ref, drc_ref)
    a_ref[...] = part if last else SHIFT * v - part


def total_of(x):
    return jnp.sum(jnp.sum(x, axis=0, keepdims=True), axis=1, keepdims=True)


def finish(rank_ref, own_ref, v_ref, part_ref, got_b_ref, v4_ref, kept_ref):
    n = own_ref.shape[1]
    size = own_ref[n : n + 1, :]
    v = v_ref[...]
    applied = part_ref[...] + where(square_mask(size), got_b_ref[...])
    v4 = SHIFT * v - applied
    v4_ref[...] = v4
    square = total_of(v4 * v4)
    top = total_of(v * applied)
    low = total_of(v * v)
    safe = jnp.maximum(square, 1e-37)
    kept_cols = jnp.minimum(jnp.full((1, n), rank_ref[0, 0].astype(f32), f32), size)
    cols = lax.broadcasted_iota(jnp.int32, (n, n), 1).astype(f32)
    kept = where(cols < jnp.broadcast_to(kept_cols, (n, n)), v4)
    kept_ref[:n, :] = kept * lax.rsqrt(safe)
    lane = lax.broadcasted_iota(jnp.int32, (8, n), 1)
    row = jnp.where(lane == 0, square, 0.0)
    row = jnp.where(lane == 1, top, row)
    row = jnp.where(lane == 2, low, row)
    row = jnp.where(lane == 3, safe, row)
    row = jnp.where(lane == 4, 1.0, row)
    kept_ref[n:, :] = row


def sums_message(own_ref, left_ref, right_ref, out_ref):
    n = own_ref.shape[1]
    lane = lax.broadcasted_iota(jnp.int32, (1, n), 1)

    def pick(ref, j):
        return jnp.sum(jnp.where(lane == j, ref[n : n + 1, :], 0.0), axis=1, keepdims=True)

    row = jnp.where(lane < 3, own_ref[n : n + 1, :], 0.0)
    row = jnp.where(lane == 3, pick(left_ref, 0), row)
    row = jnp.where(lane == 4, pick(right_ref, 0), row)
    out_ref[...] = jnp.broadcast_to(row, out_ref.shape)


def extend(left_ref, right_ref, dl_ref, hl_ref, dr_ref, hr_ref, el_ref, er_ref):
    n = left_ref.shape[1]
    kept = left_ref[:n, :]
    w = weight(kept)
    flip = kept.T
    high, low = split(flip)
    lhs = jnp.concatenate([high, low], 0)
    for c in range(el_ref.shape[0]):
        x = dl_ref[c] if c < dl_ref.shape[0] else hl_ref[c - dl_ref.shape[0]]
        xh, xl = split(x)
        half = folded(dot(jnp.concatenate([xh, xl], 1), w))
        th, tl = split(half)
        out = folded(dot(lhs, jnp.concatenate([th, tl], 1)))
        el_ref[c] = out[:n] + out[n:]
    kept = right_ref[:n, :]
    w = weight(kept.T)
    high, low = split(kept)
    lhs = jnp.concatenate([high, low], 0)
    for c in range(er_ref.shape[0]):
        y = dr_ref[c] if c < dr_ref.shape[0] else hr_ref[c - dr_ref.shape[0]]
        yh, yl = split(y.T)
        half = folded(dot(jnp.concatenate([yh, yl], 1), w))
        th, tl = split(half)
        out = folded(dot(lhs, jnp.concatenate([th, tl], 1)))
        er_ref[c] = out[:n] + out[n:]


def scaled(sums_ref, left_ref, right_ref, v4_ref, el_ref, er_ref, state_ref, lo_ref, ro_ref, energy_ref, state, lo, ro, sems):
    n = v4_ref.shape[1]
    channels = el_ref.shape[0]
    sums = jnp.sum(sums_ref[...], axis=0, keepdims=True)
    lane = lax.broadcasted_iota(jnp.int32, (1, n), 1)

    def pick(row, j):
        return jnp.sum(jnp.where(lane == j, row, 0.0), axis=1, keepdims=True)

    state[...] = v4_ref[...] * jnp.sqrt(BOND * n / pick(sums, 0))
    copies = [pltpu.make_async_copy(state, state_ref, sems.at[0])]
    copies[0].start()
    left_row, right_row = left_ref[n : n + 1, :], right_ref[n : n + 1, :]
    root = BOND * n / math.sqrt(n)
    left_scale = jnp.where(pick(left_row, 4) > 0.0, root * (pick(left_row, 3) / pick(sums, 3)), 0.0)
    right_scale = jnp.where(pick(right_row, 4) > 0.0, root * (pick(right_row, 3) / pick(sums, 4)), 0.0)
    step = 6
    for i in range(channels // step):
        at = pl.ds(i * step, step)
        lo[at] = el_ref[at] * left_scale
        copies.append(pltpu.make_async_copy(lo.at[at], lo_ref.at[at], sems.at[1 + 2 * i]))
        copies[-1].start()
        ro[at] = er_ref[at] * right_scale
        copies.append(pltpu.make_async_copy(ro.at[at], ro_ref.at[at], sems.at[2 + 2 * i]))
        copies[-1].start()
    energy_ref[0] = jnp.sum(pick(sums, 1) / pick(sums, 2))
    for copy in copies:
        copy.wait()


def call(kernel, args, specs, outs, out_specs=None, scratch=(), flops=0, name=None):
    moved = sum(math.prod(a.shape) * a.dtype.itemsize for a in (*args, *outs))
    return pl.pallas_call(
        kernel,
        in_specs=specs,
        out_specs=out_specs or [VMEM] * len(outs),
        out_shape=outs,
        scratch_shapes=list(scratch),
        compiler_params=pltpu.CompilerParams(vmem_limit_bytes=16 << 20),
        cost_estimate=pl.CostEstimate(flops=flops, bytes_accessed=moved, transcendentals=0),
        name=name,
    )(*args)


def shards(two_site, diag_left, diag_right, hop_left, hop_right, sector_sizes, ranks):
    n = two_site.shape[2]
    x0 = two_site[0, 0]
    dl, dr, hl, hr = diag_left[0, 0], diag_right[0, 0], hop_left[0, 0], hop_right[0, 0]
    hops, diags = hl.shape[0], dl.shape[0]
    blocks, segs = lax.axis_size("blk"), lax.axis_size("seg")
    up = [(i, i + 1) for i in range(blocks - 1)]
    down = [(i + 1, i) for i in range(blocks - 1)]
    seg_up = [(i, i + 1) for i in range(segs - 1)]
    seg_down = [(i + 1, i) for i in range(segs - 1)]
    block = SDS((n, n), f32)
    message = SDS((n + 8, n), f32)
    hop_parts = SDS((hops * n, 2 * n), bf16)
    diag_parts = SDS((diags * n, 2 * n), bf16)
    channel = 8 * 2 * n**3

    (own,) = call(first_message, (sector_sizes, x0), [SMEM, VMEM], [message], name="first_message")
    below0 = lax.ppermute(own, "blk", up)
    lt, rc, dlt, drc, b = call(
        first_adjoint,
        (own, hl, hr, dl, dr),
        [VMEM] * 5,
        [hop_parts, hop_parts, diag_parts, diag_parts, block],
        flops=channel * hops,
        name="first_adjoint",
    )
    got_b = lax.ppermute(b, "blk", down)
    dl_in, hl_in = lax.ppermute(dl, "seg", seg_up), lax.ppermute(hl, "seg", seg_up)
    dr_in, hr_in = lax.ppermute(dr, "seg", seg_down), lax.ppermute(hr, "seg", seg_down)
    ops = (lt, rc, dlt, drc)
    (a,) = call(first_apply, (own, below0, *ops), [VMEM] * 6, [block], flops=channel * (hops + diags), name="apply0")
    for k in range(1, ITERS):
        got_a = lax.ppermute(a, "blk", up)
        last_b = b
        v, b = call(
            adjoint, (own, a, got_b, lt, rc), [VMEM] * 5, [block, block], flops=channel * hops, name=f"adjoint{k}"
        )
        got_b = lax.ppermute(b, "blk", down)
        (a,) = call(
            functools.partial(later_apply, k == ITERS - 1),
            (own, below0, v, got_a, last_b, *ops),
            [VMEM] * 9,
            [block],
            flops=channel * (hops + diags),
            name=f"apply{k}",
        )
    v4, kept = call(finish, (ranks, own, v, a, got_b), [SMEM] + [VMEM] * 4, [block, message], name="finish")
    from_left = lax.ppermute(kept, "seg", seg_up)
    from_right = lax.ppermute(kept, "seg", seg_down)
    (sums,) = call(sums_message, (kept, from_left, from_right), [VMEM] * 3, [SDS((blocks, n), f32)], name="sums_message")
    sums = lax.all_to_all(sums, "blk", 0, 0, tiled=True)
    out = SDS((hops + diags, n, n), f32)
    el, er = call(
        extend,
        (from_left, from_right, dl_in, hl_in, dr_in, hr_in),
        [VMEM] * 6,
        [out, out],
        flops=2 * channel * (hops + diags),
        name="extend",
    )
    state, left, right, energy = call(
        scaled,
        (sums, from_left, from_right, v4, el, er),
        [VMEM] * 6,
        [block, out, out, SDS((1,), f32)],
        out_specs=[HBM, HBM, HBM, SMEM],
        scratch=[
            pltpu.VMEM((n, n), f32),
            pltpu.VMEM(out.shape, f32),
            pltpu.VMEM(out.shape, f32),
            pltpu.SemaphoreType.DMA((7,)),
        ],
        name="scaled",
    )
    return state[None, None], left[None, None], right[None, None], energy


def solution(mesh):
    wide = P("seg", "blk", None, None, None)
    return jax.shard_map(
        shards,
        mesh=mesh,
        in_specs=(P("seg", "blk", None, None), wide, wide, wide, wide, P("seg", "blk"), P("seg", "blk")),
        out_specs=(P("seg", "blk", None, None), wide, wide, P("seg")),
        check_vma=False,
    )
```

```python
import functools
import math

import jax
import jax.numpy as jnp
from jax import lax
from jax.experimental import pallas as pl
from jax.experimental.pallas import tpu as pltpu
from jax.sharding import PartitionSpec as P

ITERS = 4
SHIFT = 20.0
BOND = 6144.0
PARTS = 4
CHUNKS = 3
f32 = jnp.float32
bf16 = jnp.bfloat16
VMEM = pl.BlockSpec(memory_space=pltpu.VMEM)
SMEM = pl.BlockSpec(memory_space=pltpu.SMEM)
HBM = pl.BlockSpec(memory_space=pltpu.HBM)
ANY = pl.BlockSpec(memory_space=pl.ANY)
SDS = jax.ShapeDtypeStruct


def dot(a, b):
    return jnp.dot(a, b, preferred_element_type=f32)


def split(x):
    high = x.astype(bf16)
    return high, (x - high.astype(f32)).astype(bf16)


def weight(x):
    high, low = split(x)
    row = jnp.concatenate([high, low], 1)
    return jnp.concatenate([row, row], 0)


def folded(t):
    n = t.shape[1] // 2
    return t[:, :n] + t[:, n:]


def sandwich(p_ref, q_ref, x):
    n = x.shape[0]
    w = weight(x)
    total = None
    for pair in range(p_ref.shape[0] // (2 * n)):
        rows = pl.ds(pair * 2 * n, 2 * n)
        t = folded(dot(p_ref[rows, :], w))
        high, low = split(t)
        lhs = jnp.concatenate(
            [
                jnp.concatenate([high[:n], high[n:]], 1),
                jnp.concatenate([low[:n], low[n:]], 1),
            ],
            0,
        )
        term = dot(lhs, q_ref[rows, :])
        total = term if total is None else total + term
    total = folded(total)
    return total[:n] + total[n:]


def square_mask(size):
    n = size.shape[1]
    size = jnp.broadcast_to(size, (n, n))
    rows = lax.broadcasted_iota(jnp.int32, (n, n), 0).astype(f32)
    cols = lax.broadcasted_iota(jnp.int32, (n, n), 1).astype(f32)
    return (rows < size) & (cols < size)


def where(mask, x):
    return jnp.where(mask, x, 0.0)


def put_parts(out_ref, h, n, x):
    high, low = split(x)
    out_ref[pl.ds(h * n, n), :n] = high
    out_ref[pl.ds(h * n, n), n:] = low


def load(size_ref, x_ref, dl_ref, hl_ref, dr_ref, hr_ref, own_ref, cl_ref, cr_ref, x, sems):
    n = x.shape[0]
    diags, hops = dl_ref.shape[0], hl_ref.shape[0]
    first = pltpu.make_async_copy(x_ref, x, sems.at[0])
    first.start()
    rest = [
        pltpu.make_async_copy(dl_ref, cl_ref.at[pl.ds(0, diags)], sems.at[1]),
        pltpu.make_async_copy(dr_ref, cr_ref.at[pl.ds(0, diags)], sems.at[2]),
    ]
    part = hops // PARTS
    for i in range(PARTS):
        source, target = pl.ds(i * part, part), pl.ds(diags + i * part, part)
        rest.append(pltpu.make_async_copy(hl_ref.at[source], cl_ref.at[target], sems.at[3 + 2 * i]))
        rest.append(pltpu.make_async_copy(hr_ref.at[source], cr_ref.at[target], sems.at[4 + 2 * i]))
    for copy in rest:
        copy.start()
    first.wait()
    live = jnp.full((1, n), size_ref[0, 0].astype(f32), f32)
    own_ref[:n, :] = where(square_mask(live), x[...])
    own_ref[n:, :] = jnp.broadcast_to(live, (8, n))
    for copy in rest:
        copy.wait()


def first_adjoint(own_ref, cl_ref, cr_ref, lt_ref, rc_ref, dlt_ref, drc_ref, clt_ref, b_ref):
    n = own_ref.shape[1]
    diags = dlt_ref.shape[0] // n
    for c in range(cl_ref.shape[0]):
        flip = cl_ref[c].T
        clt_ref[c] = flip
        put_parts(dlt_ref if c < diags else lt_ref, c if c < diags else c - diags, n, flip)
        put_parts(drc_ref if c < diags else rc_ref, c if c < diags else c - diags, n, cr_ref[c])
    b_ref[...] = sandwich(lt_ref, rc_ref, own_ref[:n, :])


def adjoint(own_ref, a_ref, got_b_ref, lt_ref, rc_ref, v_ref, b_ref):
    n = own_ref.shape[1]
    v = a_ref[...] - where(square_mask(own_ref[n : n + 1, :]), got_b_ref[...])
    v_ref[...] = v
    b_ref[...] = sandwich(lt_ref, rc_ref, v)


def own_part(own_ref, v, below, lt_ref, rc_ref, dlt_ref, drc_ref):
    n = own_ref.shape[1]
    hop = sandwich(rc_ref, lt_ref, below.T)
    diag = sandwich(drc_ref, dlt_ref, v.T)
    return where(square_mask(own_ref[n : n + 1, :]), (hop + diag).T)


def first_apply(own_ref, below_ref, lt_ref, rc_ref, dlt_ref, drc_ref, a_ref):
    n = own_ref.shape[1]
    v = own_ref[:n, :]
    a_ref[...] = SHIFT * v - own_part(own_ref, v, below_ref[:n, :], lt_ref, rc_ref, dlt_ref, drc_ref)


def later_apply(last, own_ref, below_ref, v_ref, got_a_ref, b_ref, lt_ref, rc_ref, dlt_ref, drc_ref, a_ref):
    n = own_ref.shape[1]
    below = where(square_mask(below_ref[n : n + 1, :]), got_a_ref[...] - b_ref[...])
    v = v_ref[...]
    part = own_part(own_ref, v, below, lt_ref, rc_ref, dlt_ref, drc_ref)
    a_ref[...] = part if last else SHIFT * v - part


def total_of(x):
    return jnp.sum(jnp.sum(x, axis=0, keepdims=True), axis=1, keepdims=True)


def finish(rank_ref, own_ref, v_ref, part_ref, got_b_ref, v4_ref, kept_ref):
    n = own_ref.shape[1]
    size = own_ref[n : n + 1, :]
    v = v_ref[...]
    applied = part_ref[...] + where(square_mask(size), got_b_ref[...])
    v4 = SHIFT * v - applied
    v4_ref[...] = v4
    square = total_of(v4 * v4)
    top = total_of(v * applied)
    low = total_of(v * v)
    safe = jnp.maximum(square, 1e-37)
    kept_cols = jnp.minimum(jnp.full((1, n), rank_ref[0, 0].astype(f32), f32), size)
    cols = lax.broadcasted_iota(jnp.int32, (n, n), 1).astype(f32)
    kept = where(cols < jnp.broadcast_to(kept_cols, (n, n)), v4)
    kept_ref[:n, :] = kept * lax.rsqrt(safe)
    lane = lax.broadcasted_iota(jnp.int32, (8, n), 1)
    row = jnp.where(lane == 0, square, 0.0)
    row = jnp.where(lane == 1, top, row)
    row = jnp.where(lane == 2, low, row)
    row = jnp.where(lane == 3, safe, row)
    row = jnp.where(lane == 4, 1.0, row)
    kept_ref[n:, :] = row


def sums_message(own_ref, left_ref, right_ref, out_ref):
    n = own_ref.shape[1]
    lane = lax.broadcasted_iota(jnp.int32, (1, n), 1)

    def pick(ref, j):
        return jnp.sum(jnp.where(lane == j, ref[n : n + 1, :], 0.0), axis=1, keepdims=True)

    row = jnp.where(lane < 3, own_ref[n : n + 1, :], 0.0)
    row = jnp.where(lane == 3, pick(left_ref, 0), row)
    row = jnp.where(lane == 4, pick(right_ref, 0), row)
    out_ref[...] = jnp.broadcast_to(row, out_ref.shape)


def twice(x, w):
    n = x.shape[1]
    half = folded(dot(jnp.concatenate(split(x), 1), w))
    flip = jnp.concatenate([half[:n].T, half[n:].T], 0)
    return folded(dot(jnp.concatenate(split(flip), 1), w))


def extend(
    sums_ref, left_ref, right_ref, v4_ref, xl_ref, xr_ref, state_ref, lo_ref, ro_ref, energy_ref, sums, xl, xr, state, lo, ro, sems
):
    n = v4_ref.shape[1]
    channels = xl.shape[0]
    step = channels // CHUNKS
    get_sums = pltpu.make_async_copy(sums_ref, sums, sems.at[0])
    get_sums.start()
    loads, copies = [], []
    for i in range(CHUNKS):
        at = pl.ds(i * step, step)
        loads.append(pltpu.make_async_copy(xl_ref.at[at], xl.at[at], sems.at[2 + 4 * i]))
        loads.append(pltpu.make_async_copy(xr_ref.at[at], xr.at[at], sems.at[3 + 4 * i]))
    for copy in loads:
        copy.start()
    wl = weight(left_ref[:n, :])
    wr = weight(right_ref[:n, :].T)
    get_sums.wait()
    total = jnp.sum(sums[...], axis=0, keepdims=True)
    lane = lax.broadcasted_iota(jnp.int32, (1, n), 1)

    def pick(row, j):
        return jnp.sum(jnp.where(lane == j, row, 0.0), axis=1, keepdims=True)

    state[...] = v4_ref[...] * jnp.sqrt(BOND * n / pick(total, 0))
    copies.append(pltpu.make_async_copy(state, state_ref, sems.at[1]))
    copies[0].start()
    energy_ref[0] = jnp.sum(pick(total, 1) / pick(total, 2))
    left_row, right_row = left_ref[n : n + 1, :], right_ref[n : n + 1, :]
    root = BOND * n / math.sqrt(n)
    left_scale = jnp.where(pick(left_row, 4) > 0.0, root * (pick(left_row, 3) / pick(total, 3)), 0.0)
    right_scale = jnp.where(pick(right_row, 4) > 0.0, root * (pick(right_row, 3) / pick(total, 4)), 0.0)
    for i in range(CHUNKS):
        at = pl.ds(i * step, step)
        for side, (x, w, scale, out, out_ref) in enumerate(
            ((xl, wl, left_scale, lo, lo_ref), (xr, wr, right_scale, ro, ro_ref))
        ):
            loads[2 * i + side].wait()
            for c in range(i * step, (i + 1) * step, 2):
                y = twice(x[pl.ds(c, 2)].reshape(2 * n, n), w) * scale
                out[c] = y[:n]
                out[c + 1] = y[n:]
            copies.append(pltpu.make_async_copy(out.at[at], out_ref.at[at], sems.at[4 + 4 * i + side]))
            copies[-1].start()
    for copy in copies:
        copy.wait()


def call(kernel, args, specs, outs, out_specs=None, scratch=(), flops=0, limit=16, name=None):
    moved = sum(math.prod(a.shape) * a.dtype.itemsize for a in (*args, *outs))
    args = [pltpu.with_memory_space_constraint(a, pltpu.HBM) if spec is HBM else a for a, spec in zip(args, specs)]
    return pl.pallas_call(
        kernel,
        in_specs=specs,
        out_specs=out_specs or [VMEM] * len(outs),
        out_shape=outs,
        scratch_shapes=list(scratch),
        compiler_params=pltpu.CompilerParams(vmem_limit_bytes=limit << 20),
        cost_estimate=pl.CostEstimate(flops=flops, bytes_accessed=moved, transcendentals=0),
        name=name,
    )(*args)


def shards(two_site, diag_left, diag_right, hop_left, hop_right, sector_sizes, ranks):
    n = two_site.shape[2]
    x0 = two_site[0, 0]
    dl, dr, hl, hr = diag_left[0, 0], diag_right[0, 0], hop_left[0, 0], hop_right[0, 0]
    hops, diags = hl.shape[0], dl.shape[0]
    blocks, segs = lax.axis_size("blk"), lax.axis_size("seg")
    up = [(i, i + 1) for i in range(blocks - 1)]
    down = [(i + 1, i) for i in range(blocks - 1)]
    seg_up = [(i, i + 1) for i in range(segs - 1)]
    seg_down = [(i + 1, i) for i in range(segs - 1)]
    block = SDS((n, n), f32)
    message = SDS((n + 8, n), f32)
    hop_parts = SDS((hops * n, 2 * n), bf16)
    diag_parts = SDS((diags * n, 2 * n), bf16)
    out = SDS((diags + hops, n, n), f32)
    channel = 20 * 8 * 2 * n**3

    own, cl, cr = call(
        load,
        (sector_sizes, x0, dl, hl, dr, hr),
        [SMEM] + [HBM] * 5,
        [message, out, out],
        scratch=[
            pltpu.VMEM((n, n), f32),
            pltpu.SemaphoreType.DMA((3 + 2 * PARTS,)),
        ],
        limit=32,
        name="load",
    )
    below0 = lax.ppermute(own, "blk", up)
    lt, rc, dlt, drc, clt, b = call(
        first_adjoint,
        (own, cl, cr),
        [VMEM] * 3,
        [hop_parts, hop_parts, diag_parts, diag_parts, out, block],
        flops=channel * hops,
        name="first_adjoint",
    )
    got_b = lax.ppermute(b, "blk", down)
    ops = (lt, rc, dlt, drc)
    (a,) = call(first_apply, (own, below0, *ops), [VMEM] * 6, [block], flops=channel * (hops + diags), name="apply0")
    for k in range(1, ITERS):
        got_a = lax.ppermute(a, "blk", up)
        if k == 1:
            xl = lax.ppermute(lax.optimization_barrier((clt, a))[0], "seg", seg_up)
        if k == 2:
            xr = lax.ppermute(lax.optimization_barrier((cr, a))[0], "seg", seg_down)
        last_b = b
        v, b = call(
            adjoint, (own, a, got_b, lt, rc), [VMEM] * 5, [block, block], flops=channel * hops, name=f"adjoint{k}"
        )
        got_b = lax.ppermute(b, "blk", down)
        (a,) = call(
            functools.partial(later_apply, k == ITERS - 1),
            (own, below0, v, got_a, last_b, *ops),
            [VMEM] * 9,
            [block],
            flops=channel * (hops + diags),
            name=f"apply{k}",
        )
    v4, kept = call(finish, (ranks, own, v, a, got_b), [SMEM] + [VMEM] * 4, [block, message], name="finish")
    from_left = lax.ppermute(kept, "seg", seg_up)
    from_right = lax.ppermute(kept, "seg", seg_down)
    sums_block = SDS((blocks, n), f32)
    (sums,) = call(sums_message, (kept, from_left, from_right), [VMEM] * 3, [sums_block], name="sums_message")
    sums = lax.all_to_all(sums, "blk", 0, 0, tiled=True)
    state, left, right, energy = call(
        extend,
        (sums, from_left, from_right, v4, xl, xr),
        [ANY, VMEM, VMEM, VMEM, ANY, ANY],
        [block, out, out, SDS((1,), f32)],
        out_specs=[HBM, HBM, HBM, SMEM],
        scratch=[
            pltpu.VMEM(sums_block.shape, f32),
            pltpu.VMEM(out.shape, f32),
            pltpu.VMEM(out.shape, f32),
            pltpu.VMEM((n, n), f32),
            pltpu.VMEM(out.shape, f32),
            pltpu.VMEM(out.shape, f32),
            pltpu.SemaphoreType.DMA((2 + 4 * CHUNKS,)),
        ],
        flops=2 * channel * (hops + diags),
        limit=32,
        name="extend",
    )
    return state[None, None], left[None, None], right[None, None], energy


def solution(mesh):
    wide = P("seg", "blk", None, None, None)
    return jax.shard_map(
        shards,
        mesh=mesh,
        in_specs=(P("seg", "blk", None, None), wide, wide, wide, wide, P("seg", "blk"), P("seg", "blk")),
        out_specs=(P("seg", "blk", None, None), wide, wide, P("seg")),
        check_vma=False,
    )
```

```python
import functools
import math

import jax
import jax.numpy as jnp
from jax import lax
from jax.experimental import pallas as pl
from jax.experimental.pallas import tpu as pltpu
from jax.sharding import PartitionSpec as P

ITERS = 4
SHIFT = 20.0
BOND = 6144.0
PARTS = 4
CHUNKS = 3
f32 = jnp.float32
bf16 = jnp.bfloat16
VMEM = pl.BlockSpec(memory_space=pltpu.VMEM)
SMEM = pl.BlockSpec(memory_space=pltpu.SMEM)
HBM = pl.BlockSpec(memory_space=pltpu.HBM)
ANY = pl.BlockSpec(memory_space=pl.ANY)
SDS = jax.ShapeDtypeStruct


def dot(a, b):
    return jnp.dot(a, b, preferred_element_type=f32)


def split(x):
    high = x.astype(bf16)
    return high, (x - high.astype(f32)).astype(bf16)


def weight(x):
    high, low = split(x)
    row = jnp.concatenate([high, low], 1)
    return jnp.concatenate([row, row], 0)


def folded(t):
    n = t.shape[1] // 2
    return t[:, :n] + t[:, n:]


def sandwich(p_ref, q_ref, x):
    n = x.shape[0]
    w = weight(x)
    total = None
    for pair in range(p_ref.shape[0] // (2 * n)):
        rows = pl.ds(pair * 2 * n, 2 * n)
        t = folded(dot(p_ref[rows, :], w))
        high, low = split(t)
        lhs = jnp.concatenate(
            [
                jnp.concatenate([high[:n], high[n:]], 1),
                jnp.concatenate([low[:n], low[n:]], 1),
            ],
            0,
        )
        term = dot(lhs, q_ref[rows, :])
        total = term if total is None else total + term
    total = folded(total)
    return total[:n] + total[n:]


def square_mask(size):
    n = size.shape[1]
    size = jnp.broadcast_to(size, (n, n))
    rows = lax.broadcasted_iota(jnp.int32, (n, n), 0).astype(f32)
    cols = lax.broadcasted_iota(jnp.int32, (n, n), 1).astype(f32)
    return (rows < size) & (cols < size)


def where(mask, x):
    return jnp.where(mask, x, 0.0)


def put_parts(out_ref, h, n, x):
    high, low = split(x)
    out_ref[pl.ds(h * n, n), :n] = high
    out_ref[pl.ds(h * n, n), n:] = low


def load(size_ref, x_ref, dl_ref, hl_ref, dr_ref, hr_ref, own_ref, cl_ref, cr_ref, x, sems):
    n = x.shape[0]
    diags, hops = dl_ref.shape[0], hl_ref.shape[0]
    first = pltpu.make_async_copy(x_ref, x, sems.at[0])
    first.start()
    rest = [
        pltpu.make_async_copy(dl_ref, cl_ref.at[pl.ds(0, diags)], sems.at[1]),
        pltpu.make_async_copy(dr_ref, cr_ref.at[pl.ds(0, diags)], sems.at[2]),
    ]
    part = hops // PARTS
    for i in range(PARTS):
        source, target = pl.ds(i * part, part), pl.ds(diags + i * part, part)
        rest.append(pltpu.make_async_copy(hl_ref.at[source], cl_ref.at[target], sems.at[3 + 2 * i]))
        rest.append(pltpu.make_async_copy(hr_ref.at[source], cr_ref.at[target], sems.at[4 + 2 * i]))
    for copy in rest:
        copy.start()
    first.wait()
    live = jnp.full((1, n), size_ref[0, 0].astype(f32), f32)
    own_ref[:n, :] = where(square_mask(live), x[...])
    own_ref[n:, :] = jnp.broadcast_to(live, (8, n))
    for copy in rest:
        copy.wait()


def first_adjoint(own_ref, cl_ref, cr_ref, lt_ref, rc_ref, dlt_ref, drc_ref, clt_ref, b_ref):
    n = own_ref.shape[1]
    diags = dlt_ref.shape[0] // n
    for c in range(cl_ref.shape[0]):
        flip = cl_ref[c].T
        clt_ref[c] = flip
        put_parts(dlt_ref if c < diags else lt_ref, c if c < diags else c - diags, n, flip)
        put_parts(drc_ref if c < diags else rc_ref, c if c < diags else c - diags, n, cr_ref[c])
    b_ref[...] = sandwich(lt_ref, rc_ref, own_ref[:n, :])


def adjoint(own_ref, a_ref, got_b_ref, lt_ref, rc_ref, v_ref, b_ref):
    n = own_ref.shape[1]
    v = a_ref[...] - where(square_mask(own_ref[n : n + 1, :]), got_b_ref[...])
    v_ref[...] = v
    b_ref[...] = sandwich(lt_ref, rc_ref, v)


def own_part(own_ref, v, below, lt_ref, rc_ref, dlt_ref, drc_ref):
    n = own_ref.shape[1]
    hop = sandwich(rc_ref, lt_ref, below.T)
    diag = sandwich(drc_ref, dlt_ref, v.T)
    return where(square_mask(own_ref[n : n + 1, :]), (hop + diag).T)


def first_apply(own_ref, below_ref, lt_ref, rc_ref, dlt_ref, drc_ref, a_ref):
    n = own_ref.shape[1]
    v = own_ref[:n, :]
    a_ref[...] = SHIFT * v - own_part(own_ref, v, below_ref[:n, :], lt_ref, rc_ref, dlt_ref, drc_ref)


def later_apply(last, own_ref, below_ref, v_ref, got_a_ref, b_ref, lt_ref, rc_ref, dlt_ref, drc_ref, a_ref):
    n = own_ref.shape[1]
    below = where(square_mask(below_ref[n : n + 1, :]), got_a_ref[...] - b_ref[...])
    v = v_ref[...]
    part = own_part(own_ref, v, below, lt_ref, rc_ref, dlt_ref, drc_ref)
    a_ref[...] = part if last else SHIFT * v - part


def total_of(x):
    return jnp.sum(jnp.sum(x, axis=0, keepdims=True), axis=1, keepdims=True)


def finish(rank_ref, own_ref, v_ref, part_ref, got_b_ref, v4_ref, sums_ref):
    n = own_ref.shape[1]
    v = v_ref[...]
    applied = part_ref[...] + where(square_mask(own_ref[n : n + 1, :]), got_b_ref[...])
    v4 = SHIFT * v - applied
    v4_ref[:n, :] = v4
    kept_cols = jnp.minimum(jnp.full((1, n), rank_ref[0, 0].astype(f32), f32), own_ref[n : n + 1, :])
    v4_ref[n:, :] = jnp.broadcast_to(kept_cols, (8, n))
    lane = lax.broadcasted_iota(jnp.int32, (1, n), 1)
    row = jnp.where(lane == 0, total_of(v4 * v4), 0.0)
    row = jnp.where(lane == 1, total_of(v * applied), row)
    row = jnp.where(lane == 2, total_of(v * v), row)
    sums_ref[...] = jnp.broadcast_to(row, sums_ref.shape)


def normalise(v4_ref, sums_ref, state_ref, kept_ref, energy_ref):
    n = v4_ref.shape[1]
    total = jnp.sum(sums_ref[...], axis=0, keepdims=True)
    lane = lax.broadcasted_iota(jnp.int32, (1, n), 1)

    def pick(j):
        return jnp.sum(jnp.where(lane == j, total, 0.0), axis=1, keepdims=True)

    state = v4_ref[:n, :] * jnp.sqrt(BOND * n / pick(0))
    state_ref[...] = state
    cols = lax.broadcasted_iota(jnp.int32, (n, n), 1).astype(f32)
    kept_ref[...] = where(cols < jnp.broadcast_to(v4_ref[n : n + 1, :], (n, n)), state)
    energy_ref[0] = jnp.sum(pick(1) / pick(2))


def parts(xl_ref, xr_ref, pl_ref, pr_ref):
    n = xl_ref.shape[1]
    for c in range(xl_ref.shape[0]):
        put_parts(pl_ref, c, n, xl_ref[c])
        put_parts(pr_ref, c, n, xr_ref[c])


def extend(left_ref, right_ref, state_ref, pl_ref, pr_ref, new_ref, lo_ref, ro_ref, lo, ro, sems):
    n = left_ref.shape[0]
    channels = lo.shape[0]
    scale = 1.0 / math.sqrt(n)
    copies = [pltpu.make_async_copy(state_ref, new_ref, sems.at[0])]
    copies[0].start()
    sides = ((pl_ref, weight(left_ref[...]), lo, lo_ref), (pr_ref, weight(right_ref[...].T), ro, ro_ref))
    step = channels // CHUNKS
    for i in range(CHUNKS):
        at = pl.ds(i * step, step)
        for side, (x, w, out, out_ref) in enumerate(sides):
            for c in range(i * step, (i + 1) * step, 2):
                half = folded(dot(x[pl.ds(c * n, 2 * n), :], w))
                flip = jnp.concatenate([half[:n].T, half[n:].T], 0)
                y = folded(dot(jnp.concatenate(split(flip), 1), w)) * scale
                out[c] = y[:n]
                out[c + 1] = y[n:]
            copies.append(pltpu.make_async_copy(out.at[at], out_ref.at[at], sems.at[1 + 2 * i + side]))
            copies[-1].start()
    for copy in copies:
        copy.wait()


def call(kernel, args, specs, outs, out_specs=None, scratch=(), flops=0, limit=16, name=None):
    moved = sum(math.prod(a.shape) * a.dtype.itemsize for a in (*args, *outs))
    args = [pltpu.with_memory_space_constraint(a, pltpu.HBM) if spec is HBM else a for a, spec in zip(args, specs)]
    return pl.pallas_call(
        kernel,
        in_specs=specs,
        out_specs=out_specs or [VMEM] * len(outs),
        out_shape=outs,
        scratch_shapes=list(scratch),
        compiler_params=pltpu.CompilerParams(vmem_limit_bytes=limit << 20),
        cost_estimate=pl.CostEstimate(flops=flops, bytes_accessed=moved, transcendentals=0),
        name=name,
    )(*args)


def shards(two_site, diag_left, diag_right, hop_left, hop_right, sector_sizes, ranks):
    n = two_site.shape[2]
    x0 = two_site[0, 0]
    dl, dr, hl, hr = diag_left[0, 0], diag_right[0, 0], hop_left[0, 0], hop_right[0, 0]
    hops, diags = hl.shape[0], dl.shape[0]
    blocks, segs = lax.axis_size("blk"), lax.axis_size("seg")
    up = [(i, i + 1) for i in range(blocks - 1)]
    down = [(i + 1, i) for i in range(blocks - 1)]
    seg_up = [(i, i + 1) for i in range(segs - 1)]
    seg_down = [(i + 1, i) for i in range(segs - 1)]
    block = SDS((n, n), f32)
    message = SDS((n + 8, n), f32)
    hop_parts = SDS((hops * n, 2 * n), bf16)
    diag_parts = SDS((diags * n, 2 * n), bf16)
    out = SDS((diags + hops, n, n), f32)
    channel = 20 * 8 * 2 * n**3

    own, cl, cr = call(
        load,
        (sector_sizes, x0, dl, hl, dr, hr),
        [SMEM] + [HBM] * 5,
        [message, out, out],
        scratch=[
            pltpu.VMEM((n, n), f32),
            pltpu.SemaphoreType.DMA((3 + 2 * PARTS,)),
        ],
        limit=32,
        name="load",
    )
    below0 = lax.ppermute(own, "blk", up)
    lt, rc, dlt, drc, clt, b = call(
        first_adjoint,
        (own, cl, cr),
        [VMEM] * 3,
        [hop_parts, hop_parts, diag_parts, diag_parts, out, block],
        flops=channel * hops,
        name="first_adjoint",
    )
    got_b = lax.ppermute(b, "blk", down)
    ops = (lt, rc, dlt, drc)
    (a,) = call(first_apply, (own, below0, *ops), [VMEM] * 6, [block], flops=channel * (hops + diags), name="apply0")
    for k in range(1, ITERS):
        got_a = lax.ppermute(a, "blk", up)
        last_b = b
        v, b = call(
            adjoint, (own, a, got_b, lt, rc), [VMEM] * 5, [block, block], flops=channel * hops, name=f"adjoint{k}"
        )
        got_b = lax.ppermute(b, "blk", down)
        if k == ITERS - 1:
            xl = lax.ppermute(lax.optimization_barrier((clt, b))[0], "seg", seg_up)
            xr = lax.ppermute(lax.optimization_barrier((cr, b))[0], "seg", seg_down)
        (a,) = call(
            functools.partial(later_apply, k == ITERS - 1),
            (own, below0, v, got_a, last_b, *ops),
            [VMEM] * 9,
            [block],
            flops=channel * (hops + diags),
            name=f"apply{k}",
        )
    sums_block = SDS((blocks, n), f32)
    v4, sums = call(finish, (ranks, own, v, a, got_b), [SMEM] + [VMEM] * 4, [message, sums_block], name="finish")
    sums = lax.all_to_all(sums, "blk", 0, 0, tiled=True)
    state, kept, energy = call(
        normalise,
        (v4, sums),
        [VMEM] * 2,
        [block, block, SDS((1,), f32)],
        out_specs=[VMEM, VMEM, SMEM],
        name="normalise",
    )
    from_left = lax.ppermute(kept, "seg", seg_up)
    from_right = lax.ppermute(kept, "seg", seg_down)
    all_parts = SDS(((diags + hops) * n, 2 * n), bf16)
    xl, xr = call(parts, (xl, xr), [VMEM] * 2, [all_parts, all_parts], flops=channel * hops, name="parts")
    state, left, right = call(
        extend,
        (from_left, from_right, state, xl, xr),
        [VMEM] * 5,
        [block, out, out],
        out_specs=[ANY] * 3,
        scratch=[
            pltpu.VMEM(out.shape, f32),
            pltpu.VMEM(out.shape, f32),
            pltpu.SemaphoreType.DMA((1 + 2 * CHUNKS,)),
        ],
        flops=2 * channel * (hops + diags),
        name="extend",
    )
    return state[None, None], left[None, None], right[None, None], energy


def solution(mesh):
    wide = P("seg", "blk", None, None, None)
    return jax.shard_map(
        shards,
        mesh=mesh,
        in_specs=(P("seg", "blk", None, None), wide, wide, wide, wide, P("seg", "blk"), P("seg", "blk")),
        out_specs=(P("seg", "blk", None, None), wide, wide, P("seg")),
        check_vma=False,
    )
```

```python
import functools
import math

import jax
import jax.numpy as jnp
from jax import lax
from jax.experimental import pallas as pl
from jax.experimental.pallas import tpu as pltpu
from jax.sharding import PartitionSpec as P

ITERS = 4
SHIFT = 20.0
BOND = 6144.0
PARTS = 4
CHUNKS = 9
f32 = jnp.float32
bf16 = jnp.bfloat16
VMEM = pl.BlockSpec(memory_space=pltpu.VMEM)
SMEM = pl.BlockSpec(memory_space=pltpu.SMEM)
HBM = pl.BlockSpec(memory_space=pltpu.HBM)
ANY = pl.BlockSpec(memory_space=pl.ANY)
SDS = jax.ShapeDtypeStruct


def dot(a, b):
    return jnp.dot(a, b, preferred_element_type=f32)


def split(x):
    high = x.astype(bf16)
    return high, (x - high.astype(f32)).astype(bf16)


def weight(x):
    high, low = split(x)
    row = jnp.concatenate([high, low], 1)
    return jnp.concatenate([row, row], 0)


def folded(t):
    n = t.shape[1] // 2
    return t[:, :n] + t[:, n:]


def sandwich(p_ref, q_ref, x):
    n = x.shape[0]
    w = weight(x)
    total = None
    for pair in range(p_ref.shape[0] // (2 * n)):
        rows = pl.ds(pair * 2 * n, 2 * n)
        t = folded(dot(p_ref[rows, :], w))
        high, low = split(t)
        lhs = jnp.concatenate(
            [
                jnp.concatenate([high[:n], high[n:]], 1),
                jnp.concatenate([low[:n], low[n:]], 1),
            ],
            0,
        )
        term = dot(lhs, q_ref[rows, :])
        total = term if total is None else total + term
    total = folded(total)
    return total[:n] + total[n:]


def square_mask(size):
    n = size.shape[1]
    size = jnp.broadcast_to(size, (n, n))
    rows = lax.broadcasted_iota(jnp.int32, (n, n), 0).astype(f32)
    cols = lax.broadcasted_iota(jnp.int32, (n, n), 1).astype(f32)
    return (rows < size) & (cols < size)


def where(mask, x):
    return jnp.where(mask, x, 0.0)


def put_parts(out_ref, h, n, x):
    high, low = split(x)
    out_ref[pl.ds(h * n, n), :n] = high
    out_ref[pl.ds(h * n, n), n:] = low


def odd_segment():
    return lax.rem(lax.axis_index("seg"), 2) == 1


def load(size_ref, x_ref, dl_ref, hl_ref, dr_ref, hr_ref, own_ref, m0_ref, m1_ref, x, sems):
    n = x.shape[0]
    diags, hops = dl_ref.shape[0], hl_ref.shape[0]
    first = pltpu.make_async_copy(x_ref, x, sems.at[0])
    first.start()
    part = hops // PARTS
    left, right = (dl_ref, hl_ref), (dr_ref, hr_ref)

    def loads(sides):
        copies = []
        for side, ((diag, hop), out) in enumerate(zip(sides, (m0_ref, m1_ref))):
            sem = 1 + side * (1 + PARTS)
            copies.append(pltpu.make_async_copy(diag, out.at[pl.ds(0, diags)], sems.at[sem]))
            for i in range(PARTS):
                source, target = pl.ds(i * part, part), pl.ds(diags + i * part, part)
                copies.append(pltpu.make_async_copy(hop.at[source], out.at[target], sems.at[sem + 1 + i]))
        return copies

    odd = odd_segment()

    @pl.when(odd)
    def _():
        for copy in loads((right, left)):
            copy.start()

    @pl.when(jnp.logical_not(odd))
    def _():
        for copy in loads((left, right)):
            copy.start()

    first.wait()
    live = jnp.full((1, n), size_ref[0, 0].astype(f32), f32)
    own_ref[:n, :] = where(square_mask(live), x[...])
    own_ref[n:, :] = jnp.broadcast_to(live, (8, n))
    for copy in loads((left, right)):
        copy.wait()


def first_adjoint(own_ref, m0_ref, m1_ref, lt_ref, rc_ref, dlt_ref, drc_ref, b_ref):
    n = own_ref.shape[1]
    diags = dlt_ref.shape[0] // n

    def fill(left, right):
        for c in range(left.shape[0]):
            put_parts(dlt_ref if c < diags else lt_ref, c if c < diags else c - diags, n, left[c].T)
            put_parts(drc_ref if c < diags else rc_ref, c if c < diags else c - diags, n, right[c])

    odd = odd_segment()
    pl.when(odd)(lambda: fill(m1_ref, m0_ref))
    pl.when(jnp.logical_not(odd))(lambda: fill(m0_ref, m1_ref))
    b_ref[...] = sandwich(lt_ref, rc_ref, own_ref[:n, :])


def adjoint(own_ref, a_ref, got_b_ref, lt_ref, rc_ref, v_ref, b_ref):
    n = own_ref.shape[1]
    v = a_ref[...] - where(square_mask(own_ref[n : n + 1, :]), got_b_ref[...])
    v_ref[...] = v
    b_ref[...] = sandwich(lt_ref, rc_ref, v)


def own_part(own_ref, v, below, lt_ref, rc_ref, dlt_ref, drc_ref):
    n = own_ref.shape[1]
    hop = sandwich(rc_ref, lt_ref, below.T)
    diag = sandwich(drc_ref, dlt_ref, v.T)
    return where(square_mask(own_ref[n : n + 1, :]), (hop + diag).T)


def first_apply(own_ref, below_ref, lt_ref, rc_ref, dlt_ref, drc_ref, a_ref):
    n = own_ref.shape[1]
    v = own_ref[:n, :]
    a_ref[...] = SHIFT * v - own_part(own_ref, v, below_ref[:n, :], lt_ref, rc_ref, dlt_ref, drc_ref)


def later_apply(last, own_ref, below_ref, v_ref, got_a_ref, b_ref, lt_ref, rc_ref, dlt_ref, drc_ref, a_ref):
    n = own_ref.shape[1]
    below = where(square_mask(below_ref[n : n + 1, :]), got_a_ref[...] - b_ref[...])
    v = v_ref[...]
    part = own_part(own_ref, v, below, lt_ref, rc_ref, dlt_ref, drc_ref)
    a_ref[...] = part if last else SHIFT * v - part


def total_of(x):
    return jnp.sum(jnp.sum(x, axis=0, keepdims=True), axis=1, keepdims=True)


def finish(rank_ref, own_ref, v_ref, part_ref, got_b_ref, v4_ref, sums_ref):
    n = own_ref.shape[1]
    v = v_ref[...]
    applied = part_ref[...] + where(square_mask(own_ref[n : n + 1, :]), got_b_ref[...])
    v4 = SHIFT * v - applied
    v4_ref[:n, :] = v4
    kept_cols = jnp.minimum(jnp.full((1, n), rank_ref[0, 0].astype(f32), f32), own_ref[n : n + 1, :])
    v4_ref[n:, :] = jnp.broadcast_to(kept_cols, (8, n))
    lane = lax.broadcasted_iota(jnp.int32, (1, n), 1)
    row = jnp.where(lane == 0, total_of(v4 * v4), 0.0)
    row = jnp.where(lane == 1, total_of(v * applied), row)
    row = jnp.where(lane == 2, total_of(v * v), row)
    sums_ref[...] = jnp.broadcast_to(row, sums_ref.shape)


def lane_of(row, j):
    lane = lax.broadcasted_iota(jnp.int32, row.shape, 1)
    return jnp.sum(jnp.where(lane == j, row, 0.0), axis=1, keepdims=True)


def normalise(v4_ref, sums_ref, state_ref, kept_ref):
    n = v4_ref.shape[1]
    total = jnp.sum(sums_ref[...], axis=0, keepdims=True)
    state = v4_ref[:n, :] * jnp.sqrt(BOND * n / lane_of(total, 0))
    state_ref[...] = state
    cols = lax.broadcasted_iota(jnp.int32, (n, n), 1).astype(f32)
    kept_ref[...] = where(cols < jnp.broadcast_to(v4_ref[n : n + 1, :], (n, n)), state)


def parts(x0_ref, x1_ref, p0_ref, p1_ref):
    n = x0_ref.shape[1]

    def fill(left, left_out, right, right_out):
        for c in range(left.shape[0]):
            put_parts(left_out, c, n, left[c].T)
            put_parts(right_out, c, n, right[c])

    odd = odd_segment()
    pl.when(odd)(lambda: fill(x0_ref, p0_ref, x1_ref, p1_ref))
    pl.when(jnp.logical_not(odd))(lambda: fill(x1_ref, p1_ref, x0_ref, p0_ref))


def extend(is_left, kept, p_ref, left_ref, right_ref, out, sems):
    n = kept.shape[0]
    channels = out.shape[0]
    step = channels // CHUNKS
    w = weight(jnp.where(is_left, kept, kept.T))

    def copy(target, i):
        at = pl.ds(i * step, step)
        return pltpu.make_async_copy(out.at[at], target.at[at], sems.at[i])

    for i in range(CHUNKS):
        for c in range(i * step, (i + 1) * step, 2):
            half = folded(dot(p_ref[pl.ds(c * n, 2 * n), :], w))
            flip = jnp.concatenate([half[:n].T, half[n:].T], 0)
            y = folded(dot(jnp.concatenate(split(flip), 1), w)) * (1.0 / math.sqrt(n))
            out[c] = y[:n]
            out[c + 1] = y[n:]
        pl.when(is_left)(copy(left_ref, i).start)
        pl.when(jnp.logical_not(is_left))(copy(right_ref, i).start)
    for i in range(CHUNKS):
        copy(left_ref, i).wait()


def extend_first(kept_ref, p_ref, left_ref, right_ref, out, sems):
    extend(odd_segment(), kept_ref[...], p_ref, left_ref, right_ref, out, sems)


def extend_second(
    kept_ref, p_ref, state_ref, sums_ref, left_in, right_in, new_ref, left_ref, right_ref, energy_ref, out, sems, state_sem
):
    copy = pltpu.make_async_copy(state_ref, new_ref, state_sem)
    copy.start()
    total = jnp.sum(sums_ref[...], axis=0, keepdims=True)
    energy_ref[0] = jnp.sum(lane_of(total, 1) / lane_of(total, 2))
    extend(jnp.logical_not(odd_segment()), kept_ref[...], p_ref, left_ref, right_ref, out, sems)
    copy.wait()


def call(kernel, args, specs, outs, out_specs=None, scratch=(), flops=0, limit=16, aliases=None, name=None):
    moved = sum(math.prod(a.shape) * a.dtype.itemsize for a in (*args, *outs))
    args = [pltpu.with_memory_space_constraint(a, pltpu.HBM) if spec is HBM else a for a, spec in zip(args, specs)]
    return pl.pallas_call(
        kernel,
        in_specs=specs,
        out_specs=out_specs or [VMEM] * len(outs),
        out_shape=outs,
        scratch_shapes=list(scratch),
        input_output_aliases=aliases or {},
        compiler_params=pltpu.CompilerParams(vmem_limit_bytes=limit << 20),
        cost_estimate=pl.CostEstimate(flops=flops, bytes_accessed=moved, transcendentals=0),
        name=name,
    )(*args)


def shards(two_site, diag_left, diag_right, hop_left, hop_right, sector_sizes, ranks):
    n = two_site.shape[2]
    x0 = two_site[0, 0]
    dl, dr, hl, hr = diag_left[0, 0], diag_right[0, 0], hop_left[0, 0], hop_right[0, 0]
    hops, diags = hl.shape[0], dl.shape[0]
    blocks, segs = lax.axis_size("blk"), lax.axis_size("seg")
    up = [(i, i + 1) for i in range(blocks - 1)]
    down = [(i + 1, i) for i in range(blocks - 1)]
    chip = [(i, i ^ 1) for i in range(segs)]
    across = [(i, i + 1) for i in range(1, segs - 1, 2)]
    across += [(target, source) for source, target in across]
    block = SDS((n, n), f32)
    message = SDS((n + 8, n), f32)
    hop_parts = SDS((hops * n, 2 * n), bf16)
    diag_parts = SDS((diags * n, 2 * n), bf16)
    out = SDS((diags + hops, n, n), f32)
    channel = 20 * 8 * 2 * n**3

    own, m0, m1 = call(
        load,
        (sector_sizes, x0, dl, hl, dr, hr),
        [SMEM] + [HBM] * 5,
        [message, out, out],
        scratch=[
            pltpu.VMEM((n, n), f32),
            pltpu.SemaphoreType.DMA((3 + 2 * PARTS,)),
        ],
        limit=32,
        name="load",
    )
    below0 = lax.ppermute(own, "blk", up)
    lt, rc, dlt, drc, b = call(
        first_adjoint,
        (own, m0, m1),
        [VMEM] * 3,
        [hop_parts, hop_parts, diag_parts, diag_parts, block],
        flops=channel * hops,
        name="first_adjoint",
    )
    got_b = lax.ppermute(b, "blk", down)
    ops = (lt, rc, dlt, drc)
    (a,) = call(first_apply, (own, below0, *ops), [VMEM] * 6, [block], flops=channel * (hops + diags), name="apply0")
    for k in range(1, ITERS):
        got_a = lax.ppermute(a, "blk", up)
        last_b = b
        v, b = call(
            adjoint, (own, a, got_b, lt, rc), [VMEM] * 5, [block, block], flops=channel * hops, name=f"adjoint{k}"
        )
        got_b = lax.ppermute(b, "blk", down)
        if k == ITERS - 1:
            x1 = lax.ppermute(lax.optimization_barrier((m1, b))[0], "seg", across)
            x0 = lax.ppermute(lax.optimization_barrier((m0, b))[0], "seg", chip)
        (a,) = call(
            functools.partial(later_apply, k == ITERS - 1),
            (own, below0, v, got_a, last_b, *ops),
            [VMEM] * 9,
            [block],
            flops=channel * (hops + diags),
            name=f"apply{k}",
        )
    sums_block = SDS((blocks, n), f32)
    v4, sums = call(finish, (ranks, own, v, a, got_b), [SMEM] + [VMEM] * 4, [message, sums_block], name="finish")
    sums = lax.all_to_all(sums, "blk", 0, 0, tiled=True)
    state, kept = call(normalise, (v4, sums), [VMEM] * 2, [block, block], name="normalise")
    kept1 = lax.ppermute(kept, "seg", across)
    kept0 = lax.ppermute(kept, "seg", chip)
    all_parts = SDS(((diags + hops) * n, 2 * n), bf16)
    p0, p1 = call(parts, (x0, x1), [VMEM] * 2, [all_parts, all_parts], flops=channel * hops, name="parts")
    rooms = [pltpu.VMEM(out.shape, f32), pltpu.SemaphoreType.DMA((CHUNKS,))]
    left, right = call(
        extend_first,
        (kept0, p0),
        [VMEM] * 2,
        [out, out],
        out_specs=[ANY] * 2,
        scratch=rooms,
        flops=channel * (hops + diags),
        name="extend_first",
    )
    state, left, right, energy = call(
        extend_second,
        (kept1, p1, state, sums, left, right),
        [VMEM] * 4 + [ANY] * 2,
        [block, out, out, SDS((1,), f32)],
        out_specs=[ANY] * 3 + [SMEM],
        scratch=[*rooms, pltpu.SemaphoreType.DMA],
        flops=channel * (hops + diags),
        aliases={4: 1, 5: 2},
        name="extend_second",
    )
    return state[None, None], left[None, None], right[None, None], energy


def solution(mesh):
    wide = P("seg", "blk", None, None, None)
    return jax.shard_map(
        shards,
        mesh=mesh,
        in_specs=(P("seg", "blk", None, None), wide, wide, wide, wide, P("seg", "blk"), P("seg", "blk")),
        out_specs=(P("seg", "blk", None, None), wide, wide, P("seg")),
        check_vma=False,
    )
```

```python
import functools
import math

import jax
import jax.numpy as jnp
from jax import lax
from jax.experimental import pallas as pl
from jax.experimental.pallas import tpu as pltpu
from jax.sharding import PartitionSpec as P

ITERS = 4
SHIFT = 20.0
BOND = 6144.0
PARTS = 4
CHUNKS = 3
f32 = jnp.float32
bf16 = jnp.bfloat16
VMEM = pl.BlockSpec(memory_space=pltpu.VMEM)
SMEM = pl.BlockSpec(memory_space=pltpu.SMEM)
HBM = pl.BlockSpec(memory_space=pltpu.HBM)
ANY = pl.BlockSpec(memory_space=pl.ANY)
SDS = jax.ShapeDtypeStruct


def dot(a, b):
    return jnp.dot(a, b, preferred_element_type=f32)


def split(x):
    high = x.astype(bf16)
    return high, (x - high.astype(f32)).astype(bf16)


def weight(x):
    high, low = split(x)
    row = jnp.concatenate([high, low], 1)
    return jnp.concatenate([row, row], 0)


def folded(t):
    n = t.shape[1] // 2
    return t[:, :n] + t[:, n:]


def sandwich(p_ref, q_ref, x):
    n = x.shape[0]
    w = weight(x)
    total = None
    for pair in range(p_ref.shape[0] // (2 * n)):
        rows = pl.ds(pair * 2 * n, 2 * n)
        t = folded(dot(p_ref[rows, :], w))
        high, low = split(t)
        lhs = jnp.concatenate(
            [
                jnp.concatenate([high[:n], high[n:]], 1),
                jnp.concatenate([low[:n], low[n:]], 1),
            ],
            0,
        )
        term = dot(lhs, q_ref[rows, :])
        total = term if total is None else total + term
    total = folded(total)
    return total[:n] + total[n:]


def square_mask(size):
    n = size.shape[1]
    size = jnp.broadcast_to(size, (n, n))
    rows = lax.broadcasted_iota(jnp.int32, (n, n), 0).astype(f32)
    cols = lax.broadcasted_iota(jnp.int32, (n, n), 1).astype(f32)
    return (rows < size) & (cols < size)


def where(mask, x):
    return jnp.where(mask, x, 0.0)


def put_parts(out_ref, h, n, x):
    high, low = split(x)
    out_ref[pl.ds(h * n, n), :n] = high
    out_ref[pl.ds(h * n, n), n:] = low


def odd(axis):
    return lax.rem(lax.axis_index(axis), 2) == 1


def load(size_ref, x_ref, dl_ref, hl_ref, dr_ref, hr_ref, own_ref, m0_ref, m1_ref, x, sems):
    n = x.shape[0]
    diags, hops = dl_ref.shape[0], hl_ref.shape[0]
    first = pltpu.make_async_copy(x_ref, x, sems.at[0])
    first.start()
    part = hops // PARTS
    left, right = (dl_ref, hl_ref), (dr_ref, hr_ref)

    def loads(sides):
        copies = []
        for side, ((diag, hop), out) in enumerate(zip(sides, (m0_ref, m1_ref))):
            sem = 1 + side * (1 + PARTS)
            copies.append(pltpu.make_async_copy(diag, out.at[pl.ds(0, diags)], sems.at[sem]))
            for i in range(PARTS):
                source, target = pl.ds(i * part, part), pl.ds(diags + i * part, part)
                copies.append(pltpu.make_async_copy(hop.at[source], out.at[target], sems.at[sem + 1 + i]))
        return copies

    segment = odd("seg")

    @pl.when(segment)
    def _():
        for copy in loads((right, left)):
            copy.start()

    @pl.when(jnp.logical_not(segment))
    def _():
        for copy in loads((left, right)):
            copy.start()

    first.wait()
    live = jnp.full((1, n), size_ref[0, 0].astype(f32), f32)
    own_ref[:n, :] = where(square_mask(live), x[...])
    own_ref[n:, :] = jnp.broadcast_to(live, (8, n))
    for copy in loads((left, right)):
        copy.wait()


def messages(low_ref, high_ref, up, down):
    n = up.shape[0]
    sector = odd("blk")
    low_ref[:n, :] = jnp.where(sector, down, up)
    high_ref[:n, :] = jnp.where(sector, up, down)


def received(low_ref, high_ref):
    n = low_ref.shape[1]
    low, high = low_ref[:n, :], high_ref[:n, :]
    sector = odd("blk")
    return jnp.where(sector, low, high), jnp.where(sector, high, low)


def sent_down(low_ref, high_ref):
    n = low_ref.shape[1]
    return jnp.where(odd("blk"), low_ref[:n, :], high_ref[:n, :])


def first_adjoint(own_ref, m0_ref, m1_ref, lt_ref, rc_ref, dlt_ref, drc_ref, low_ref, high_ref):
    n = own_ref.shape[1]
    diags = dlt_ref.shape[0] // n
    segment = odd("seg")
    for c in range(m0_ref.shape[0]):
        x, y = m0_ref[c], m1_ref[c]
        k = c if c < diags else c - diags
        put_parts(dlt_ref if c < diags else lt_ref, k, n, jnp.where(segment, y, x).T)
        put_parts(drc_ref if c < diags else rc_ref, k, n, jnp.where(segment, x, y))
    v = own_ref[:n, :]
    messages(low_ref, high_ref, v, sandwich(lt_ref, rc_ref, v))
    low_ref[n:, :] = own_ref[n:, :]
    high_ref[n:, :] = own_ref[n:, :]


def applied_here(size, v, below, lt_ref, rc_ref, dlt_ref, drc_ref):
    hop = sandwich(rc_ref, lt_ref, below.T)
    diag = sandwich(drc_ref, dlt_ref, v.T)
    return where(square_mask(size), (hop + diag).T)


def first_round(own_ref, high_in, low_in, lt_ref, rc_ref, dlt_ref, drc_ref, size_ref, v_ref, low_ref, high_ref):
    n = own_ref.shape[1]
    size = own_ref[n : n + 1, :]
    below, above = received(low_in, high_in)
    size_ref[...] = jnp.where(odd("blk"), low_in[n:, :], high_in[n:, :])
    v = own_ref[:n, :]
    a = SHIFT * v - applied_here(size, v, below, lt_ref, rc_ref, dlt_ref, drc_ref)
    v = a - where(square_mask(size), above)
    v_ref[...] = v
    messages(low_ref, high_ref, a, sandwich(lt_ref, rc_ref, v))


def later_round(
    own_ref, v_ref, high_in, low_in, low_sent, high_sent, size_ref, lt_ref, rc_ref, dlt_ref, drc_ref, new_ref, low_ref, high_ref
):
    n = own_ref.shape[1]
    size = own_ref[n : n + 1, :]
    below, above = received(low_in, high_in)
    below = where(square_mask(size_ref[0:1, :]), below - sent_down(low_sent, high_sent))
    v = v_ref[...]
    a = SHIFT * v - applied_here(size, v, below, lt_ref, rc_ref, dlt_ref, drc_ref)
    v = a - where(square_mask(size), above)
    new_ref[...] = v
    messages(low_ref, high_ref, a, sandwich(lt_ref, rc_ref, v))


def total_of(x):
    return jnp.sum(jnp.sum(x, axis=0, keepdims=True), axis=1, keepdims=True)


def last_round(
    rank_ref, own_ref, v_ref, high_in, low_in, low_sent, high_sent, size_ref, lt_ref, rc_ref, dlt_ref, drc_ref, v4_ref, sums_ref
):
    n = own_ref.shape[1]
    size = own_ref[n : n + 1, :]
    below, above = received(low_in, high_in)
    below = where(square_mask(size_ref[0:1, :]), below - sent_down(low_sent, high_sent))
    v = v_ref[...]
    applied = applied_here(size, v, below, lt_ref, rc_ref, dlt_ref, drc_ref) + where(square_mask(size), above)
    v4 = SHIFT * v - applied
    v4_ref[:n, :] = v4
    kept_cols = jnp.minimum(jnp.full((1, n), rank_ref[0, 0].astype(f32), f32), size)
    v4_ref[n:, :] = jnp.broadcast_to(kept_cols, (8, n))
    lane = lax.broadcasted_iota(jnp.int32, (1, n), 1)
    row = jnp.where(lane == 0, total_of(v4 * v4), 0.0)
    row = jnp.where(lane == 1, total_of(v * applied), row)
    row = jnp.where(lane == 2, total_of(v * v), row)
    sums_ref[...] = jnp.broadcast_to(row, sums_ref.shape)


def lane_of(row, j):
    lane = lax.broadcasted_iota(jnp.int32, row.shape, 1)
    return jnp.sum(jnp.where(lane == j, row, 0.0), axis=1, keepdims=True)


def normalise(v4_ref, sums_ref, state_ref, kept_ref):
    n = v4_ref.shape[1]
    total = jnp.sum(sums_ref[...], axis=0, keepdims=True)
    state = v4_ref[:n, :] * jnp.sqrt(BOND * n / lane_of(total, 0))
    state_ref[...] = state
    cols = lax.broadcasted_iota(jnp.int32, (n, n), 1).astype(f32)
    kept_ref[...] = where(cols < jnp.broadcast_to(v4_ref[n : n + 1, :], (n, n)), state)


def parts(x0_ref, x1_ref, sums_ref, p0_ref, p1_ref, energy_ref):
    n = x0_ref.shape[1]
    segment = odd("seg")
    for c in range(x0_ref.shape[0]):
        x, y = x0_ref[c], x1_ref[c]
        put_parts(p0_ref, c, n, jnp.where(segment, x.T, x))
        put_parts(p1_ref, c, n, jnp.where(segment, y, y.T))
    total = jnp.sum(sums_ref[...], axis=0, keepdims=True)
    energy_ref[0] = jnp.sum(lane_of(total, 1) / lane_of(total, 2))


def extend(
    kept1_ref, kept0_ref, p0_ref, p1_ref, state_ref, new_ref, left_ref, right_ref, out0, out1, sems, state_sem
):
    n = kept0_ref.shape[0]
    channels = out0.shape[0]
    step = channels // CHUNKS
    segment = odd("seg")
    even = jnp.logical_not(segment)
    state_copy = pltpu.make_async_copy(state_ref, new_ref, state_sem)
    state_copy.start()
    sides = []
    for side, (kept_ref, p_ref, out, is_left) in enumerate(
        ((kept0_ref, p0_ref, out0, segment), (kept1_ref, p1_ref, out1, even))
    ):
        kept = kept_ref[...]
        sides.append((side, p_ref, out, weight(jnp.where(is_left, kept, kept.T))))

    def copy(side, target, i):
        at = pl.ds(i * step, step)
        return pltpu.make_async_copy((out0, out1)[side].at[at], target.at[at], sems.at[side, i])

    for i in range(CHUNKS):
        for side, p_ref, out, w in sides:
            for c in range(i * step, (i + 1) * step, 2):
                half = folded(dot(p_ref[pl.ds(c * n, 2 * n), :], w))
                flip = jnp.concatenate([half[:n].T, half[n:].T], 0)
                y = folded(dot(jnp.concatenate(split(flip), 1), w)) * (1.0 / math.sqrt(n))
                out[c] = y[:n]
                out[c + 1] = y[n:]

        @pl.when(segment)
        def _():
            copy(0, left_ref, i).start()
            copy(1, right_ref, i).start()

        @pl.when(even)
        def _():
            copy(0, right_ref, i).start()
            copy(1, left_ref, i).start()

    for i in range(CHUNKS):
        copy(0, left_ref, i).wait()
        copy(1, right_ref, i).wait()
    state_copy.wait()


def call(kernel, args, specs, outs, out_specs=None, scratch=(), flops=0, limit=16, name=None):
    moved = sum(math.prod(a.shape) * a.dtype.itemsize for a in (*args, *outs))
    args = [pltpu.with_memory_space_constraint(a, pltpu.HBM) if spec is HBM else a for a, spec in zip(args, specs)]
    return pl.pallas_call(
        kernel,
        in_specs=specs,
        out_specs=out_specs or [VMEM] * len(outs),
        out_shape=outs,
        scratch_shapes=list(scratch),
        compiler_params=pltpu.CompilerParams(vmem_limit_bytes=limit << 20),
        cost_estimate=pl.CostEstimate(flops=flops, bytes_accessed=moved, transcendentals=0),
        name=name,
    )(*args)


def shards(two_site, diag_left, diag_right, hop_left, hop_right, sector_sizes, ranks):
    n = two_site.shape[2]
    x0 = two_site[0, 0]
    dl, dr, hl, hr = diag_left[0, 0], diag_right[0, 0], hop_left[0, 0], hop_right[0, 0]
    hops, diags = hl.shape[0], dl.shape[0]
    blocks, segs = lax.axis_size("blk"), lax.axis_size("seg")
    low_pairs = [(i, i ^ 1) for i in range(blocks)]
    high_pairs = [(i, i + 1) for i in range(1, blocks - 1, 2)]
    high_pairs += [(target, source) for source, target in high_pairs]
    chip = [(i, i ^ 1) for i in range(segs)]
    across = [(i, i + 1) for i in range(1, segs - 1, 2)]
    across += [(target, source) for source, target in across]
    block = SDS((n, n), f32)
    message = SDS((n + 8, n), f32)
    hop_parts = SDS((hops * n, 2 * n), bf16)
    diag_parts = SDS((diags * n, 2 * n), bf16)
    out = SDS((diags + hops, n, n), f32)
    channel = 20 * 8 * 2 * n**3

    own, m0, m1 = call(
        load,
        (sector_sizes, x0, dl, hl, dr, hr),
        [SMEM] + [HBM] * 5,
        [message, out, out],
        scratch=[
            pltpu.VMEM((n, n), f32),
            pltpu.SemaphoreType.DMA((3 + 2 * PARTS,)),
        ],
        limit=32,
        name="load",
    )
    lt, rc, dlt, drc, low, high = call(
        first_adjoint,
        (own, m0, m1),
        [VMEM] * 3,
        [hop_parts, hop_parts, diag_parts, diag_parts, message, message],
        flops=channel * hops,
        name="first_adjoint",
    )
    ops = (lt, rc, dlt, drc)
    for k in range(ITERS):
        high_in = lax.ppermute(high, "blk", high_pairs)
        low_in = lax.ppermute(low, "blk", low_pairs)
        sent = low, high
        if k == 0:
            size, v, low, high = call(
                first_round,
                (own, high_in, low_in, *ops),
                [VMEM] * 7,
                [SDS((8, n), f32), block, block, block],
                flops=channel * (2 * hops + diags),
                name="round0",
            )
        elif k < ITERS - 1:
            v, low, high = call(
                later_round,
                (own, v, high_in, low_in, *before, size, *ops),
                [VMEM] * 11,
                [block, block, block],
                flops=channel * (2 * hops + diags),
                name=f"round{k}",
            )
        if k < ITERS - 1:
            before = sent
    x1 = lax.ppermute(lax.optimization_barrier((m1, sent[0]))[0], "seg", across)
    x0 = lax.ppermute(lax.optimization_barrier((m0, sent[0]))[0], "seg", chip)
    sums_block = SDS((blocks, n), f32)
    v4, sums = call(
        last_round,
        (lax.optimization_barrier((ranks, sent[0]))[0], own, v, high_in, low_in, *before, size, *ops),
        [SMEM] + [VMEM] * 11,
        [message, sums_block],
        flops=channel * (hops + diags),
        name="last_round",
    )
    sums = lax.all_to_all(sums, "blk", 0, 0, tiled=True)
    state, kept = call(normalise, (v4, sums), [VMEM] * 2, [block, block], name="normalise")
    kept1 = lax.ppermute(kept, "seg", across)
    kept0 = lax.ppermute(kept, "seg", chip)
    all_parts = SDS(((diags + hops) * n, 2 * n), bf16)
    p0, p1, energy = call(
        parts,
        (x0, x1, sums),
        [VMEM] * 3,
        [all_parts, all_parts, SDS((1,), f32)],
        out_specs=[VMEM, VMEM, SMEM],
        flops=channel * hops,
        name="parts",
    )
    state, left, right = call(
        extend,
        (kept1, kept0, p0, p1, state),
        [VMEM] * 5,
        [block, out, out],
        out_specs=[ANY] * 3,
        scratch=[
            pltpu.VMEM(out.shape, f32),
            pltpu.VMEM(out.shape, f32),
            pltpu.SemaphoreType.DMA((2, CHUNKS)),
            pltpu.SemaphoreType.DMA,
        ],
        flops=2 * channel * (hops + diags),
        name="extend",
    )
    return state[None, None], left[None, None], right[None, None], energy


def solution(mesh):
    wide = P("seg", "blk", None, None, None)
    return jax.shard_map(
        shards,
        mesh=mesh,
        in_specs=(P("seg", "blk", None, None), wide, wide, wide, wide, P("seg", "blk"), P("seg", "blk")),
        out_specs=(P("seg", "blk", None, None), wide, wide, P("seg")),
        check_vma=False,
    )
```

```python
import functools
import math

import jax
import jax.numpy as jnp
from jax import lax
from jax.experimental import pallas as pl
from jax.experimental.pallas import tpu as pltpu
from jax.sharding import PartitionSpec as P

ITERS = 4
SHIFT = 20.0
BOND = 6144.0
PARTS = 4
CHUNKS = 3
f32 = jnp.float32
bf16 = jnp.bfloat16
VMEM = pl.BlockSpec(memory_space=pltpu.VMEM)
SMEM = pl.BlockSpec(memory_space=pltpu.SMEM)
HBM = pl.BlockSpec(memory_space=pltpu.HBM)
ANY = pl.BlockSpec(memory_space=pl.ANY)
SDS = jax.ShapeDtypeStruct


def dot(a, b):
    return jnp.dot(a, b, preferred_element_type=f32)


def split(x):
    high = x.astype(bf16)
    return high, (x - high.astype(f32)).astype(bf16)


def weight(x):
    high, low = split(x)
    row = jnp.concatenate([high, low], 1)
    return jnp.concatenate([row, row], 0)


def folded(t):
    n = t.shape[1] // 2
    return t[:, :n] + t[:, n:]


def sandwich(p_ref, q_ref, x):
    n = x.shape[0]
    w = weight(x)
    total = None
    for pair in range(p_ref.shape[0] // (2 * n)):
        rows = pl.ds(pair * 2 * n, 2 * n)
        t = folded(dot(p_ref[rows, :], w))
        high, low = split(t)
        lhs = jnp.concatenate(
            [
                jnp.concatenate([high[:n], high[n:]], 1),
                jnp.concatenate([low[:n], low[n:]], 1),
            ],
            0,
        )
        term = dot(lhs, q_ref[rows, :])
        total = term if total is None else total + term
    total = folded(total)
    return total[:n] + total[n:]


def square_mask(size):
    n = size.shape[1]
    size = jnp.broadcast_to(size, (n, n))
    rows = lax.broadcasted_iota(jnp.int32, (n, n), 0).astype(f32)
    cols = lax.broadcasted_iota(jnp.int32, (n, n), 1).astype(f32)
    return (rows < size) & (cols < size)


def where(mask, x):
    return jnp.where(mask, x, 0.0)


def put_parts(out_ref, h, n, x):
    high, low = split(x)
    out_ref[pl.ds(h * n, n), :n] = high
    out_ref[pl.ds(h * n, n), n:] = low


def odd(axis):
    return lax.rem(lax.axis_index(axis), 2) == 1


def load(size_ref, x_ref, dl_ref, hl_ref, dr_ref, hr_ref, own_ref, m0_ref, m1_ref, x, sems):
    n = x.shape[0]
    diags, hops = dl_ref.shape[0], hl_ref.shape[0]
    first = pltpu.make_async_copy(x_ref, x, sems.at[0])
    first.start()
    part = hops // PARTS
    left, right = (dl_ref, hl_ref), (dr_ref, hr_ref)

    def loads(sides):
        copies = []
        for side, ((diag, hop), out) in enumerate(zip(sides, (m0_ref, m1_ref))):
            sem = 1 + side * (1 + PARTS)
            copies.append(pltpu.make_async_copy(diag, out.at[pl.ds(0, diags)], sems.at[sem]))
            for i in range(PARTS):
                source, target = pl.ds(i * part, part), pl.ds(diags + i * part, part)
                copies.append(pltpu.make_async_copy(hop.at[source], out.at[target], sems.at[sem + 1 + i]))
        return copies

    segment = odd("seg")

    @pl.when(segment)
    def _():
        for copy in loads((right, left)):
            copy.start()

    @pl.when(jnp.logical_not(segment))
    def _():
        for copy in loads((left, right)):
            copy.start()

    first.wait()
    live = jnp.full((1, n), size_ref[0, 0].astype(f32), f32)
    own_ref[:n, :] = where(square_mask(live), x[...])
    own_ref[n:, :] = jnp.broadcast_to(live, (8, n))
    for copy in loads((left, right)):
        copy.wait()


def first_adjoint(own_ref, m0_ref, m1_ref, lt_ref, rc_ref, dlt_ref, drc_ref, b_ref):
    n = own_ref.shape[1]
    diags = dlt_ref.shape[0] // n
    segment = odd("seg")
    for c in range(m0_ref.shape[0]):
        x, y = m0_ref[c], m1_ref[c]
        k = c if c < diags else c - diags
        put_parts(dlt_ref if c < diags else lt_ref, k, n, jnp.where(segment, y, x).T)
        put_parts(drc_ref if c < diags else rc_ref, k, n, jnp.where(segment, x, y))
    b_ref[...] = sandwich(lt_ref, rc_ref, own_ref[:n, :])


def adjoint(own_ref, a_ref, got_b_ref, lt_ref, rc_ref, v_ref, b_ref):
    n = own_ref.shape[1]
    v = a_ref[...] - where(square_mask(own_ref[n : n + 1, :]), got_b_ref[...])
    v_ref[...] = v
    b_ref[...] = sandwich(lt_ref, rc_ref, v)


def own_part(own_ref, v, below, lt_ref, rc_ref, dlt_ref, drc_ref):
    n = own_ref.shape[1]
    hop = sandwich(rc_ref, lt_ref, below.T)
    diag = sandwich(drc_ref, dlt_ref, v.T)
    return where(square_mask(own_ref[n : n + 1, :]), (hop + diag).T)


def first_apply(own_ref, below_ref, lt_ref, rc_ref, dlt_ref, drc_ref, a_ref):
    n = own_ref.shape[1]
    v = own_ref[:n, :]
    a_ref[...] = SHIFT * v - own_part(own_ref, v, below_ref[:n, :], lt_ref, rc_ref, dlt_ref, drc_ref)


def later_apply(last, own_ref, below_ref, v_ref, got_a_ref, b_ref, lt_ref, rc_ref, dlt_ref, drc_ref, a_ref):
    n = own_ref.shape[1]
    below = where(square_mask(below_ref[n : n + 1, :]), got_a_ref[...] - b_ref[...])
    v = v_ref[...]
    part = own_part(own_ref, v, below, lt_ref, rc_ref, dlt_ref, drc_ref)
    a_ref[...] = part if last else SHIFT * v - part


def total_of(x):
    return jnp.sum(jnp.sum(x, axis=0, keepdims=True), axis=1, keepdims=True)


def finish(rank_ref, own_ref, v_ref, part_ref, got_b_ref, v4_ref, sums_ref):
    n = own_ref.shape[1]
    v = v_ref[...]
    applied = part_ref[...] + where(square_mask(own_ref[n : n + 1, :]), got_b_ref[...])
    v4 = SHIFT * v - applied
    v4_ref[:n, :] = v4
    kept_cols = jnp.minimum(jnp.full((1, n), rank_ref[0, 0].astype(f32), f32), own_ref[n : n + 1, :])
    v4_ref[n:, :] = jnp.broadcast_to(kept_cols, (8, n))
    lane = lax.broadcasted_iota(jnp.int32, (1, n), 1)
    row = jnp.where(lane == 0, total_of(v4 * v4), 0.0)
    row = jnp.where(lane == 1, total_of(v * applied), row)
    row = jnp.where(lane == 2, total_of(v * v), row)
    sums_ref[...] = jnp.broadcast_to(row, sums_ref.shape)


def lane_of(row, j):
    lane = lax.broadcasted_iota(jnp.int32, row.shape, 1)
    return jnp.sum(jnp.where(lane == j, row, 0.0), axis=1, keepdims=True)


def normalise(v4_ref, sums_ref, state_ref, kept_ref):
    n = v4_ref.shape[1]
    total = jnp.sum(sums_ref[...], axis=0, keepdims=True)
    state = v4_ref[:n, :] * jnp.sqrt(BOND * n / lane_of(total, 0))
    state_ref[...] = state
    cols = lax.broadcasted_iota(jnp.int32, (n, n), 1).astype(f32)
    kept_ref[...] = where(cols < jnp.broadcast_to(v4_ref[n : n + 1, :], (n, n)), state)


def parts(x0_ref, x1_ref, sums_ref, p0_ref, p1_ref, energy_ref):
    n = x0_ref.shape[1]
    segment = odd("seg")
    for c in range(x0_ref.shape[0]):
        x, y = x0_ref[c], x1_ref[c]
        put_parts(p0_ref, c, n, jnp.where(segment, x.T, x))
        put_parts(p1_ref, c, n, jnp.where(segment, y, y.T))
    total = jnp.sum(sums_ref[...], axis=0, keepdims=True)
    energy_ref[0] = jnp.sum(lane_of(total, 1) / lane_of(total, 2))


def extend(
    kept1_ref, kept0_ref, p0_ref, p1_ref, state_ref, new_ref, left_ref, right_ref, out0, out1, sems, state_sem
):
    n = kept0_ref.shape[0]
    channels = out0.shape[0]
    step = channels // CHUNKS
    segment = odd("seg")
    even = jnp.logical_not(segment)
    state_copy = pltpu.make_async_copy(state_ref, new_ref, state_sem)
    state_copy.start()
    sides = []
    for side, (kept_ref, p_ref, out, is_left) in enumerate(
        ((kept0_ref, p0_ref, out0, segment), (kept1_ref, p1_ref, out1, even))
    ):
        kept = kept_ref[...]
        sides.append((side, p_ref, out, weight(jnp.where(is_left, kept, kept.T))))

    def copy(side, target, i):
        at = pl.ds(i * step, step)
        return pltpu.make_async_copy((out0, out1)[side].at[at], target.at[at], sems.at[side, i])

    for i in range(CHUNKS):
        for side, p_ref, out, w in sides:
            for c in range(i * step, (i + 1) * step, 2):
                half = folded(dot(p_ref[pl.ds(c * n, 2 * n), :], w))
                flip = jnp.concatenate([half[:n].T, half[n:].T], 0)
                y = folded(dot(jnp.concatenate(split(flip), 1), w)) * (1.0 / math.sqrt(n))
                out[c] = y[:n]
                out[c + 1] = y[n:]

        @pl.when(segment)
        def _():
            copy(0, left_ref, i).start()
            copy(1, right_ref, i).start()

        @pl.when(even)
        def _():
            copy(0, right_ref, i).start()
            copy(1, left_ref, i).start()

    for i in range(CHUNKS):
        copy(0, left_ref, i).wait()
        copy(1, right_ref, i).wait()
    state_copy.wait()


def call(kernel, args, specs, outs, out_specs=None, scratch=(), flops=0, limit=16, name=None):
    moved = sum(math.prod(a.shape) * a.dtype.itemsize for a in (*args, *outs))
    args = [pltpu.with_memory_space_constraint(a, pltpu.HBM) if spec is HBM else a for a, spec in zip(args, specs)]
    return pl.pallas_call(
        kernel,
        in_specs=specs,
        out_specs=out_specs or [VMEM] * len(outs),
        out_shape=outs,
        scratch_shapes=list(scratch),
        compiler_params=pltpu.CompilerParams(vmem_limit_bytes=limit << 20),
        cost_estimate=pl.CostEstimate(flops=flops, bytes_accessed=moved, transcendentals=0),
        name=name,
    )(*args)


def shards(two_site, diag_left, diag_right, hop_left, hop_right, sector_sizes, ranks):
    n = two_site.shape[2]
    x0 = two_site[0, 0]
    dl, dr, hl, hr = diag_left[0, 0], diag_right[0, 0], hop_left[0, 0], hop_right[0, 0]
    hops, diags = hl.shape[0], dl.shape[0]
    blocks, segs = lax.axis_size("blk"), lax.axis_size("seg")
    up = [(i, i + 1) for i in range(blocks - 1)]
    down = [(i + 1, i) for i in range(blocks - 1)]
    chip = [(i, i ^ 1) for i in range(segs)]
    across = [(i, i + 1) for i in range(1, segs - 1, 2)]
    across += [(target, source) for source, target in across]
    block = SDS((n, n), f32)
    message = SDS((n + 8, n), f32)
    hop_parts = SDS((hops * n, 2 * n), bf16)
    diag_parts = SDS((diags * n, 2 * n), bf16)
    out = SDS((diags + hops, n, n), f32)
    channel = 20 * 8 * 2 * n**3

    own, m0, m1 = call(
        load,
        (sector_sizes, x0, dl, hl, dr, hr),
        [SMEM] + [HBM] * 5,
        [message, out, out],
        scratch=[
            pltpu.VMEM((n, n), f32),
            pltpu.SemaphoreType.DMA((3 + 2 * PARTS,)),
        ],
        limit=32,
        name="load",
    )
    below0 = lax.ppermute(own, "blk", up)
    lt, rc, dlt, drc, b = call(
        first_adjoint,
        (own, m0, m1),
        [VMEM] * 3,
        [hop_parts, hop_parts, diag_parts, diag_parts, block],
        flops=channel * hops,
        name="first_adjoint",
    )
    got_b = lax.ppermute(b, "blk", down)
    ops = (lt, rc, dlt, drc)
    (a,) = call(first_apply, (own, below0, *ops), [VMEM] * 6, [block], flops=channel * (hops + diags), name="apply0")
    for k in range(1, ITERS):
        got_a = lax.ppermute(a, "blk", up)
        last_b = b
        v, b = call(
            adjoint, (own, a, got_b, lt, rc), [VMEM] * 5, [block, block], flops=channel * hops, name=f"adjoint{k}"
        )
        got_b = lax.ppermute(b, "blk", down)
        if k == ITERS - 1:
            x1 = lax.ppermute(lax.optimization_barrier((m1, b))[0], "seg", across)
            x0 = lax.ppermute(lax.optimization_barrier((m0, b))[0], "seg", chip)
        (a,) = call(
            functools.partial(later_apply, k == ITERS - 1),
            (own, below0, v, got_a, last_b, *ops),
            [VMEM] * 9,
            [block],
            flops=channel * (hops + diags),
            name=f"apply{k}",
        )
    sums_block = SDS((blocks, n), f32)
    v4, sums = call(finish, (ranks, own, v, a, got_b), [SMEM] + [VMEM] * 4, [message, sums_block], name="finish")
    members = [(i + blocks // 2 + blocks // 16) % blocks for i in range(blocks)]
    sums = lax.all_to_all(sums, "blk", 0, 0, tiled=True, axis_index_groups=[members])
    state, kept = call(normalise, (v4, sums), [VMEM] * 2, [block, block], name="normalise")
    kept1 = lax.ppermute(kept, "seg", across)
    kept0 = lax.ppermute(kept, "seg", chip)
    all_parts = SDS(((diags + hops) * n, 2 * n), bf16)
    p0, p1, energy = call(
        parts,
        (x0, x1, sums),
        [VMEM] * 3,
        [all_parts, all_parts, SDS((1,), f32)],
        out_specs=[VMEM, VMEM, SMEM],
        flops=channel * hops,
        name="parts",
    )
    state, left, right = call(
        extend,
        (kept1, kept0, p0, p1, state),
        [VMEM] * 5,
        [block, out, out],
        out_specs=[ANY] * 3,
        scratch=[
            pltpu.VMEM(out.shape, f32),
            pltpu.VMEM(out.shape, f32),
            pltpu.SemaphoreType.DMA((2, CHUNKS)),
            pltpu.SemaphoreType.DMA,
        ],
        flops=2 * channel * (hops + diags),
        name="extend",
    )
    return state[None, None], left[None, None], right[None, None], energy


def solution(mesh):
    wide = P("seg", "blk", None, None, None)
    return jax.shard_map(
        shards,
        mesh=mesh,
        in_specs=(P("seg", "blk", None, None), wide, wide, wide, wide, P("seg", "blk"), P("seg", "blk")),
        out_specs=(P("seg", "blk", None, None), wide, wide, P("seg")),
        check_vma=False,
    )
```

```python
import functools
import math

import jax
import jax.numpy as jnp
from jax import lax
from jax.experimental import pallas as pl
from jax.experimental.pallas import tpu as pltpu
from jax.sharding import PartitionSpec as P

ITERS = 4
SHIFT = 20.0
BOND = 6144.0
PARTS = 4
CHUNKS = 3
f32 = jnp.float32
bf16 = jnp.bfloat16
VMEM = pl.BlockSpec(memory_space=pltpu.VMEM)
SMEM = pl.BlockSpec(memory_space=pltpu.SMEM)
HBM = pl.BlockSpec(memory_space=pltpu.HBM)
ANY = pl.BlockSpec(memory_space=pl.ANY)
SDS = jax.ShapeDtypeStruct


def dot(a, b):
    return jnp.dot(a, b, preferred_element_type=f32)


def split(x):
    high = x.astype(bf16)
    return high, (x - high.astype(f32)).astype(bf16)


def weight(x):
    high, low = split(x)
    row = jnp.concatenate([high, low], 1)
    return jnp.concatenate([row, row], 0)


def folded(t):
    n = t.shape[1] // 2
    return t[:, :n] + t[:, n:]


def sandwich(p_ref, q_ref, x):
    n = x.shape[0]
    w = weight(x)
    total = None
    for pair in range(p_ref.shape[0] // (2 * n)):
        rows = pl.ds(pair * 2 * n, 2 * n)
        t = folded(dot(p_ref[rows, :], w))
        high, low = split(t)
        lhs = jnp.concatenate(
            [
                jnp.concatenate([high[:n], high[n:]], 1),
                jnp.concatenate([low[:n], low[n:]], 1),
            ],
            0,
        )
        term = dot(lhs, q_ref[rows, :])
        total = term if total is None else total + term
    total = folded(total)
    return total[:n] + total[n:]


def square_mask(size):
    n = size.shape[1]
    size = jnp.broadcast_to(size, (n, n))
    rows = lax.broadcasted_iota(jnp.int32, (n, n), 0).astype(f32)
    cols = lax.broadcasted_iota(jnp.int32, (n, n), 1).astype(f32)
    return (rows < size) & (cols < size)


def where(mask, x):
    return jnp.where(mask, x, 0.0)


def put_parts(out_ref, h, n, x):
    high, low = split(x)
    out_ref[pl.ds(h * n, n), :n] = high
    out_ref[pl.ds(h * n, n), n:] = low


def odd(axis):
    return lax.rem(lax.axis_index(axis), 2) == 1


def load(size_ref, x_ref, dl_ref, hl_ref, dr_ref, hr_ref, own_ref, m0_ref, m1_ref, x, sems):
    n = x.shape[0]
    diags, hops = dl_ref.shape[0], hl_ref.shape[0]
    first = pltpu.make_async_copy(x_ref, x, sems.at[0])
    first.start()
    part = hops // PARTS
    left, right = (dl_ref, hl_ref), (dr_ref, hr_ref)

    def loads(sides):
        copies = []
        for side, ((diag, hop), out) in enumerate(zip(sides, (m0_ref, m1_ref))):
            sem = 1 + side * (1 + PARTS)
            copies.append(pltpu.make_async_copy(diag, out.at[pl.ds(0, diags)], sems.at[sem]))
            for i in range(PARTS):
                source, target = pl.ds(i * part, part), pl.ds(diags + i * part, part)
                copies.append(pltpu.make_async_copy(hop.at[source], out.at[target], sems.at[sem + 1 + i]))
        return copies

    segment = odd("seg")

    @pl.when(segment)
    def _():
        for copy in loads((right, left)):
            copy.start()

    @pl.when(jnp.logical_not(segment))
    def _():
        for copy in loads((left, right)):
            copy.start()

    first.wait()
    live = jnp.full((1, n), size_ref[0, 0].astype(f32), f32)
    own_ref[:n, :] = where(square_mask(live), x[...])
    own_ref[n:, :] = jnp.broadcast_to(live, (8, n))
    for copy in loads((left, right)):
        copy.wait()


def first_product(own_ref, m0_ref, m1_ref, lt_ref, rc_ref, dlt_ref, drc_ref, b_ref):
    n = own_ref.shape[1]
    diags = dlt_ref.shape[0] // n
    segment = odd("seg")
    for c in range(m0_ref.shape[0]):
        x, y = m0_ref[c], m1_ref[c]
        k = c if c < diags else c - diags
        put_parts(dlt_ref if c < diags else lt_ref, k, n, jnp.where(segment, y, x).T)
        put_parts(drc_ref if c < diags else rc_ref, k, n, jnp.where(segment, x, y))
    b_ref[...] = sandwich(lt_ref, rc_ref, own_ref[:n, :])


def odd_adjoint(*refs):
    pl.when(odd("blk"))(lambda: first_product(*refs))


def even_adjoint(own_ref, m0_ref, m1_ref, done_ref, lt_ref, rc_ref, dlt_ref, drc_ref, b_ref):
    @pl.when(odd("blk"))
    def _():
        b_ref[...] = done_ref[...]

    @pl.when(jnp.logical_not(odd("blk")))
    def _():
        first_product(own_ref, m0_ref, m1_ref, lt_ref, rc_ref, dlt_ref, drc_ref, b_ref)


def by_parity(kernel, count):
    def chosen(*refs):
        odd_ops, even_ops, rest = refs[:count], refs[count : 2 * count], refs[2 * count :]
        pl.when(odd("blk"))(lambda: kernel(*odd_ops, *rest))
        pl.when(jnp.logical_not(odd("blk")))(lambda: kernel(*even_ops, *rest))

    return chosen


def adjoint(lt_ref, rc_ref, own_ref, a_ref, got_b_ref, v_ref, b_ref):
    n = own_ref.shape[1]
    v = a_ref[...] - where(square_mask(own_ref[n : n + 1, :]), got_b_ref[...])
    v_ref[...] = v
    b_ref[...] = sandwich(lt_ref, rc_ref, v)


def own_part(own_ref, v, below, lt_ref, rc_ref, dlt_ref, drc_ref):
    n = own_ref.shape[1]
    hop = sandwich(rc_ref, lt_ref, below.T)
    diag = sandwich(drc_ref, dlt_ref, v.T)
    return where(square_mask(own_ref[n : n + 1, :]), (hop + diag).T)


def first_apply(lt_ref, rc_ref, dlt_ref, drc_ref, own_ref, below_ref, a_ref):
    n = own_ref.shape[1]
    v = own_ref[:n, :]
    a_ref[...] = SHIFT * v - own_part(own_ref, v, below_ref[:n, :], lt_ref, rc_ref, dlt_ref, drc_ref)


def later_apply(last, lt_ref, rc_ref, dlt_ref, drc_ref, own_ref, below_ref, v_ref, got_a_ref, b_ref, a_ref):
    n = own_ref.shape[1]
    below = where(square_mask(below_ref[n : n + 1, :]), got_a_ref[...] - b_ref[...])
    v = v_ref[...]
    part = own_part(own_ref, v, below, lt_ref, rc_ref, dlt_ref, drc_ref)
    a_ref[...] = part if last else SHIFT * v - part


def total_of(x):
    return jnp.sum(jnp.sum(x, axis=0, keepdims=True), axis=1, keepdims=True)


def finish(rank_ref, own_ref, v_ref, part_ref, got_b_ref, v4_ref, sums_ref):
    n = own_ref.shape[1]
    v = v_ref[...]
    applied = part_ref[...] + where(square_mask(own_ref[n : n + 1, :]), got_b_ref[...])
    v4 = SHIFT * v - applied
    v4_ref[:n, :] = v4
    kept_cols = jnp.minimum(jnp.full((1, n), rank_ref[0, 0].astype(f32), f32), own_ref[n : n + 1, :])
    v4_ref[n:, :] = jnp.broadcast_to(kept_cols, (8, n))
    lane = lax.broadcasted_iota(jnp.int32, (1, n), 1)
    row = jnp.where(lane == 0, total_of(v4 * v4), 0.0)
    row = jnp.where(lane == 1, total_of(v * applied), row)
    row = jnp.where(lane == 2, total_of(v * v), row)
    sums_ref[...] = jnp.broadcast_to(row, sums_ref.shape)


def lane_of(row, j):
    lane = lax.broadcasted_iota(jnp.int32, row.shape, 1)
    return jnp.sum(jnp.where(lane == j, row, 0.0), axis=1, keepdims=True)


def normalise(v4_ref, sums_ref, state_ref, kept_ref):
    n = v4_ref.shape[1]
    total = jnp.sum(sums_ref[...], axis=0, keepdims=True)
    state = v4_ref[:n, :] * jnp.sqrt(BOND * n / lane_of(total, 0))
    state_ref[...] = state
    cols = lax.broadcasted_iota(jnp.int32, (n, n), 1).astype(f32)
    kept_ref[...] = where(cols < jnp.broadcast_to(v4_ref[n : n + 1, :], (n, n)), state)


def parts(x0_ref, x1_ref, sums_ref, pl_ref, pr_ref, energy_ref):
    n = x0_ref.shape[1]
    segment = odd("seg")
    for c in range(x0_ref.shape[0]):
        x, y = x0_ref[c], x1_ref[c]
        put_parts(pl_ref, c, n, jnp.where(segment, x, y).T)
        put_parts(pr_ref, c, n, jnp.where(segment, y, x))
    total = jnp.sum(sums_ref[...], axis=0, keepdims=True)
    energy_ref[0] = jnp.sum(lane_of(total, 1) / lane_of(total, 2))


def extend(kept1_ref, kept0_ref, pl_ref, pr_ref, state_ref, new_ref, left_ref, right_ref, lo, ro, sems):
    n = kept0_ref.shape[0]
    step = lo.shape[0] // CHUNKS
    copies = [pltpu.make_async_copy(state_ref, new_ref, sems.at[0])]
    copies[0].start()
    segment = odd("seg")
    x, y = kept0_ref[...], kept1_ref[...]
    sides = (
        (pl_ref, weight(jnp.where(segment, x, y)), lo, left_ref),
        (pr_ref, weight(jnp.where(segment, y, x).T), ro, right_ref),
    )
    for i in range(CHUNKS):
        at = pl.ds(i * step, step)
        for side, (p_ref, w, out, target) in enumerate(sides):
            for c in range(i * step, (i + 1) * step, 2):
                half = folded(dot(p_ref[pl.ds(c * n, 2 * n), :], w))
                flip = jnp.concatenate([half[:n].T, half[n:].T], 0)
                z = folded(dot(jnp.concatenate(split(flip), 1), w)) * (1.0 / math.sqrt(n))
                out[c] = z[:n]
                out[c + 1] = z[n:]
            copies.append(pltpu.make_async_copy(out.at[at], target.at[at], sems.at[1 + 2 * i + side]))
            copies[-1].start()
    for copy in copies:
        copy.wait()


def call(kernel, args, specs, outs, out_specs=None, scratch=(), flops=0, limit=16, name=None):
    moved = sum(math.prod(a.shape) * a.dtype.itemsize for a in (*args, *outs))
    args = [pltpu.with_memory_space_constraint(a, pltpu.HBM) if spec is HBM else a for a, spec in zip(args, specs)]
    return pl.pallas_call(
        kernel,
        in_specs=specs,
        out_specs=out_specs or [VMEM] * len(outs),
        out_shape=outs,
        scratch_shapes=list(scratch),
        compiler_params=pltpu.CompilerParams(vmem_limit_bytes=limit << 20),
        cost_estimate=pl.CostEstimate(flops=flops, bytes_accessed=moved, transcendentals=0),
        name=name,
    )(*args)


def shards(two_site, diag_left, diag_right, hop_left, hop_right, sector_sizes, ranks):
    n = two_site.shape[2]
    x0 = two_site[0, 0]
    dl, dr, hl, hr = diag_left[0, 0], diag_right[0, 0], hop_left[0, 0], hop_right[0, 0]
    hops, diags = hl.shape[0], dl.shape[0]
    blocks, segs = lax.axis_size("blk"), lax.axis_size("seg")
    up = [(i, i + 1) for i in range(blocks - 1)]
    down = [(i + 1, i) for i in range(blocks - 1)]
    chip = [(i, i ^ 1) for i in range(segs)]
    across = [(i, i + 1) for i in range(1, segs - 1, 2)]
    across += [(target, source) for source, target in across]
    block = SDS((n, n), f32)
    message = SDS((n + 8, n), f32)
    hop_parts = SDS((hops * n, 2 * n), bf16)
    diag_parts = SDS((diags * n, 2 * n), bf16)
    out = SDS((diags + hops, n, n), f32)
    channel = 20 * 8 * 2 * n**3

    own, m0, m1 = call(
        load,
        (sector_sizes, x0, dl, hl, dr, hr),
        [SMEM] + [HBM] * 5,
        [message, out, out],
        scratch=[
            pltpu.VMEM((n, n), f32),
            pltpu.SemaphoreType.DMA((3 + 2 * PARTS,)),
        ],
        limit=32,
        name="load",
    )
    products = [hop_parts, hop_parts, diag_parts, diag_parts, block]
    *odd_ops, b = call(odd_adjoint, (own, m0, m1), [VMEM] * 3, products, flops=channel * hops, name="odd_adjoint")
    below0 = lax.ppermute(lax.optimization_barrier((own, b))[0], "blk", up)
    *even_ops, b = call(
        even_adjoint, (own, m0, m1, b), [VMEM] * 4, products, flops=channel * hops, name="even_adjoint"
    )
    got_b = lax.ppermute(b, "blk", down)
    ops = (*odd_ops, *even_ops)
    hop_ops = (*odd_ops[:2], *even_ops[:2])
    (a,) = call(
        by_parity(first_apply, 4),
        (*ops, own, below0),
        [VMEM] * 10,
        [block],
        flops=channel * (hops + diags),
        name="apply0",
    )
    for k in range(1, ITERS):
        got_a = lax.ppermute(a, "blk", up)
        last_b = b
        v, b = call(
            by_parity(adjoint, 2),
            (*hop_ops, own, a, got_b),
            [VMEM] * 7,
            [block, block],
            flops=channel * hops,
            name=f"adjoint{k}",
        )
        got_b = lax.ppermute(b, "blk", down)
        if k == ITERS - 1:
            x1 = lax.ppermute(lax.optimization_barrier((m1, b))[0], "seg", across)
            x0 = lax.ppermute(lax.optimization_barrier((m0, b))[0], "seg", chip)
        (a,) = call(
            by_parity(functools.partial(later_apply, k == ITERS - 1), 4),
            (*ops, own, below0, v, got_a, last_b),
            [VMEM] * 13,
            [block],
            flops=channel * (hops + diags),
            name=f"apply{k}",
        )
    sums_block = SDS((blocks, n), f32)
    v4, sums = call(finish, (ranks, own, v, a, got_b), [SMEM] + [VMEM] * 4, [message, sums_block], name="finish")
    members = [(i + blocks // 2 + blocks // 16) % blocks for i in range(blocks)]
    sums = lax.all_to_all(sums, "blk", 0, 0, tiled=True, axis_index_groups=[members])
    state, kept = call(normalise, (v4, sums), [VMEM] * 2, [block, block], name="normalise")
    kept1 = lax.ppermute(kept, "seg", across)
    kept0 = lax.ppermute(kept, "seg", chip)
    all_parts = SDS(((diags + hops) * n, 2 * n), bf16)
    p0, p1, energy = call(
        parts,
        (x0, x1, sums),
        [VMEM] * 3,
        [all_parts, all_parts, SDS((1,), f32)],
        out_specs=[VMEM, VMEM, SMEM],
        flops=channel * hops,
        name="parts",
    )
    state, left, right = call(
        extend,
        (kept1, kept0, p0, p1, state),
        [VMEM] * 5,
        [block, out, out],
        out_specs=[ANY] * 3,
        scratch=[
            pltpu.VMEM(out.shape, f32),
            pltpu.VMEM(out.shape, f32),
            pltpu.SemaphoreType.DMA((1 + 2 * CHUNKS,)),
        ],
        flops=2 * channel * (hops + diags),
        name="extend",
    )
    return state[None, None], left[None, None], right[None, None], energy


def solution(mesh):
    wide = P("seg", "blk", None, None, None)
    return jax.shard_map(
        shards,
        mesh=mesh,
        in_specs=(P("seg", "blk", None, None), wide, wide, wide, wide, P("seg", "blk"), P("seg", "blk")),
        out_specs=(P("seg", "blk", None, None), wide, wide, P("seg")),
        check_vma=False,
    )
```

```python
import functools
import math

import jax
import jax.numpy as jnp
from jax import lax
from jax.experimental import pallas as pl
from jax.experimental.pallas import tpu as pltpu
from jax.sharding import PartitionSpec as P

ITERS = 4
SHIFT = 20.0
BOND = 6144.0
PARTS = 4
CHUNKS = 3
f32 = jnp.float32
bf16 = jnp.bfloat16
VMEM = pl.BlockSpec(memory_space=pltpu.VMEM)
SMEM = pl.BlockSpec(memory_space=pltpu.SMEM)
HBM = pl.BlockSpec(memory_space=pltpu.HBM)
ANY = pl.BlockSpec(memory_space=pl.ANY)
SDS = jax.ShapeDtypeStruct


def dot(a, b):
    return jnp.dot(a, b, preferred_element_type=f32)


def split(x):
    high = x.astype(bf16)
    return high, (x - high.astype(f32)).astype(bf16)


def weight(x):
    high, low = split(x)
    row = jnp.concatenate([high, low], 1)
    return jnp.concatenate([row, row], 0)


def folded(t):
    n = t.shape[1] // 2
    return t[:, :n] + t[:, n:]


def sandwich(p_ref, q_ref, x):
    n = x.shape[0]
    w = weight(x)
    total = None
    for pair in range(p_ref.shape[0] // (2 * n)):
        rows = pl.ds(pair * 2 * n, 2 * n)
        t = folded(dot(p_ref[rows, :], w))
        high, low = split(t)
        lhs = jnp.concatenate(
            [
                jnp.concatenate([high[:n], high[n:]], 1),
                jnp.concatenate([low[:n], low[n:]], 1),
            ],
            0,
        )
        term = dot(lhs, q_ref[rows, :])
        total = term if total is None else total + term
    total = folded(total)
    return total[:n] + total[n:]


def square_mask(size):
    n = size.shape[1]
    size = jnp.broadcast_to(size, (n, n))
    rows = lax.broadcasted_iota(jnp.int32, (n, n), 0).astype(f32)
    cols = lax.broadcasted_iota(jnp.int32, (n, n), 1).astype(f32)
    return (rows < size) & (cols < size)


def where(mask, x):
    return jnp.where(mask, x, 0.0)


def put_parts(out_ref, h, n, x):
    high, low = split(x)
    out_ref[pl.ds(h * n, n), :n] = high
    out_ref[pl.ds(h * n, n), n:] = low


def odd(axis):
    return lax.rem(lax.axis_index(axis), 2) == 1


def first_message(size_ref, x_ref, own_ref, x, sem):
    n = x.shape[0]
    copy = pltpu.make_async_copy(x_ref, x, sem)
    copy.start()
    copy.wait()
    live = jnp.full((1, n), size_ref[0, 0].astype(f32), f32)
    own_ref[:n, :] = where(square_mask(live), x[...])
    own_ref[n:, :] = jnp.broadcast_to(live, (8, n))


def joined(sides, outs, sems):
    copies = []
    for side, ((diag, hop), out) in enumerate(zip(sides, outs)):
        diags, part = diag.shape[0], hop.shape[0] // PARTS
        copies.append(pltpu.make_async_copy(diag, out.at[pl.ds(0, diags)], sems.at[side, PARTS]))
        for i in range(PARTS):
            source, target = pl.ds(i * part, part), pl.ds(diags + i * part, part)
            copies.append(pltpu.make_async_copy(hop.at[source], out.at[target], sems.at[side, i]))
    return copies


def first_product(own_ref, dl_ref, hl_ref, dr_ref, hr_ref, lt_ref, rc_ref, dlt_ref, drc_ref, b_ref, left, right, sems):
    n = own_ref.shape[1]
    diags = dl_ref.shape[0]
    copies = joined(((dl_ref, hl_ref), (dr_ref, hr_ref)), (left, right), sems)
    for copy in copies:
        copy.start()
    for copy in copies:
        copy.wait()
    for c in range(left.shape[0]):
        k = c if c < diags else c - diags
        put_parts(dlt_ref if c < diags else lt_ref, k, n, left[c].T)
        put_parts(drc_ref if c < diags else rc_ref, k, n, right[c])
    b_ref[...] = sandwich(lt_ref, rc_ref, own_ref[:n, :])


def odd_adjoint(*refs):
    pl.when(odd("blk"))(lambda: first_product(*refs))


def even_adjoint(done_ref, own_ref, dl_ref, hl_ref, dr_ref, hr_ref, lt_ref, rc_ref, dlt_ref, drc_ref, b_ref, d_ref, *scratch):
    n = own_ref.shape[1]

    @pl.when(odd("blk"))
    def _():
        b_ref[...] = done_ref[...]

    @pl.when(jnp.logical_not(odd("blk")))
    def _():
        first_product(own_ref, dl_ref, hl_ref, dr_ref, hr_ref, lt_ref, rc_ref, dlt_ref, drc_ref, b_ref, *scratch)
        d_ref[...] = sandwich(drc_ref, dlt_ref, own_ref[:n, :].T)


def gather(dl_ref, hl_ref, dr_ref, hr_ref, outs, sems):
    left, right = (dl_ref, hl_ref), (dr_ref, hr_ref)
    segment = odd("seg")

    @pl.when(segment)
    def _():
        for copy in joined((right, left), outs, sems):
            copy.start()

    @pl.when(jnp.logical_not(segment))
    def _():
        for copy in joined((left, right), outs, sems):
            copy.start()

    for copy in joined((left, right), outs, sems):
        copy.wait()


def odd_gather(after_ref, dl_ref, hl_ref, dr_ref, hr_ref, m0_ref, m1_ref, sems):
    pl.when(odd("blk"))(lambda: gather(dl_ref, hl_ref, dr_ref, hr_ref, (m0_ref, m1_ref), sems))


def even_gather(after_ref, dl_ref, hl_ref, dr_ref, hr_ref, m0_in, m1_in, m0_ref, m1_ref, sems):
    even = jnp.logical_not(odd("blk"))
    pl.when(even)(lambda: gather(dl_ref, hl_ref, dr_ref, hr_ref, (m0_ref, m1_ref), sems))


def by_parity(kernel):
    def chosen(*refs):
        pl.when(odd("blk"))(lambda: kernel(True, refs[:4], *refs[8:]))
        pl.when(jnp.logical_not(odd("blk")))(lambda: kernel(False, refs[4:8], *refs[8:]))

    return chosen


def adjoint(is_odd, ops, own_ref, a_ref, got_b_ref, v_ref, b_ref, d_ref):
    lt_ref, rc_ref, dlt_ref, drc_ref = ops
    n = own_ref.shape[1]
    v = a_ref[...] - where(square_mask(own_ref[n : n + 1, :]), got_b_ref[...])
    v_ref[...] = v
    b_ref[...] = sandwich(lt_ref, rc_ref, v)
    if not is_odd:
        d_ref[...] = sandwich(drc_ref, dlt_ref, v.T)


def own_part(is_odd, ops, own_ref, v, below, d_ref):
    lt_ref, rc_ref, dlt_ref, drc_ref = ops
    n = own_ref.shape[1]
    diag = sandwich(drc_ref, dlt_ref, v.T) if is_odd else d_ref[...]
    return where(square_mask(own_ref[n : n + 1, :]), (sandwich(rc_ref, lt_ref, below.T) + diag).T)


def first_apply(is_odd, ops, own_ref, below_ref, d_ref, a_ref):
    n = own_ref.shape[1]
    v = own_ref[:n, :]
    a_ref[...] = SHIFT * v - own_part(is_odd, ops, own_ref, v, below_ref[:n, :], d_ref)


def later_apply(last, is_odd, ops, own_ref, below_ref, v_ref, d_ref, got_a_ref, b_ref, a_ref):
    n = own_ref.shape[1]
    below = where(square_mask(below_ref[n : n + 1, :]), got_a_ref[...] - b_ref[...])
    v = v_ref[...]
    part = own_part(is_odd, ops, own_ref, v, below, d_ref)
    a_ref[...] = part if last else SHIFT * v - part


def total_of(x):
    return jnp.sum(jnp.sum(x, axis=0, keepdims=True), axis=1, keepdims=True)


def finish(rank_ref, own_ref, v_ref, part_ref, got_b_ref, v4_ref, sums_ref):
    n = own_ref.shape[1]
    v = v_ref[...]
    applied = part_ref[...] + where(square_mask(own_ref[n : n + 1, :]), got_b_ref[...])
    v4 = SHIFT * v - applied
    v4_ref[:n, :] = v4
    kept_cols = jnp.minimum(jnp.full((1, n), rank_ref[0, 0].astype(f32), f32), own_ref[n : n + 1, :])
    v4_ref[n:, :] = jnp.broadcast_to(kept_cols, (8, n))
    lane = lax.broadcasted_iota(jnp.int32, (1, n), 1)
    row = jnp.where(lane == 0, total_of(v4 * v4), 0.0)
    row = jnp.where(lane == 1, total_of(v * applied), row)
    row = jnp.where(lane == 2, total_of(v * v), row)
    sums_ref[...] = jnp.broadcast_to(row, sums_ref.shape)


def lane_of(row, j):
    lane = lax.broadcasted_iota(jnp.int32, row.shape, 1)
    return jnp.sum(jnp.where(lane == j, row, 0.0), axis=1, keepdims=True)


def normalise(v4_ref, sums_ref, state_ref, kept_ref):
    n = v4_ref.shape[1]
    total = jnp.sum(sums_ref[...], axis=0, keepdims=True)
    state = v4_ref[:n, :] * jnp.sqrt(BOND * n / lane_of(total, 0))
    state_ref[...] = state
    cols = lax.broadcasted_iota(jnp.int32, (n, n), 1).astype(f32)
    kept_ref[...] = where(cols < jnp.broadcast_to(v4_ref[n : n + 1, :], (n, n)), state)


def parts(x0_ref, x1_ref, sums_ref, pl_ref, pr_ref, energy_ref):
    n = x0_ref.shape[1]
    segment = odd("seg")
    for c in range(x0_ref.shape[0]):
        x, y = x0_ref[c], x1_ref[c]
        put_parts(pl_ref, c, n, jnp.where(segment, x, y).T)
        put_parts(pr_ref, c, n, jnp.where(segment, y, x))
    total = jnp.sum(sums_ref[...], axis=0, keepdims=True)
    energy_ref[0] = jnp.sum(lane_of(total, 1) / lane_of(total, 2))


def extend(kept1_ref, kept0_ref, pl_ref, pr_ref, state_ref, new_ref, left_ref, right_ref, lo, ro, sems):
    n = kept0_ref.shape[0]
    step = lo.shape[0] // CHUNKS
    copies = [pltpu.make_async_copy(state_ref, new_ref, sems.at[0])]
    copies[0].start()
    segment = odd("seg")
    x, y = kept0_ref[...], kept1_ref[...]
    sides = (
        (pl_ref, weight(jnp.where(segment, x, y)), lo, left_ref),
        (pr_ref, weight(jnp.where(segment, y, x).T), ro, right_ref),
    )
    for i in range(CHUNKS):
        at = pl.ds(i * step, step)
        for side, (p_ref, w, out, target) in enumerate(sides):
            for c in range(i * step, (i + 1) * step, 2):
                half = folded(dot(p_ref[pl.ds(c * n, 2 * n), :], w))
                flip = jnp.concatenate([half[:n].T, half[n:].T], 0)
                z = folded(dot(jnp.concatenate(split(flip), 1), w)) * (1.0 / math.sqrt(n))
                out[c] = z[:n]
                out[c + 1] = z[n:]
            copies.append(pltpu.make_async_copy(out.at[at], target.at[at], sems.at[1 + 2 * i + side]))
            copies[-1].start()
    for copy in copies:
        copy.wait()


def call(kernel, args, specs, outs, out_specs=None, scratch=(), flops=0, limit=16, aliases=None, name=None):
    moved = sum(math.prod(a.shape) * a.dtype.itemsize for a in (*args, *outs))
    args = [pltpu.with_memory_space_constraint(a, pltpu.HBM) if spec is HBM else a for a, spec in zip(args, specs)]
    return pl.pallas_call(
        kernel,
        in_specs=specs,
        out_specs=out_specs or [VMEM] * len(outs),
        out_shape=outs,
        scratch_shapes=list(scratch),
        input_output_aliases=aliases or {},
        compiler_params=pltpu.CompilerParams(vmem_limit_bytes=limit << 20),
        cost_estimate=pl.CostEstimate(flops=flops, bytes_accessed=moved, transcendentals=0),
        name=name,
    )(*args)


def shards(two_site, diag_left, diag_right, hop_left, hop_right, sector_sizes, ranks):
    n = two_site.shape[2]
    x0 = two_site[0, 0]
    dl, dr, hl, hr = diag_left[0, 0], diag_right[0, 0], hop_left[0, 0], hop_right[0, 0]
    hops, diags = hl.shape[0], dl.shape[0]
    blocks, segs = lax.axis_size("blk"), lax.axis_size("seg")
    up = [(i, i + 1) for i in range(blocks - 1)]
    down = [(i + 1, i) for i in range(blocks - 1)]
    chip = [(i, i ^ 1) for i in range(segs)]
    across = [(i, i + 1) for i in range(1, segs - 1, 2)]
    across += [(target, source) for source, target in across]
    block = SDS((n, n), f32)
    message = SDS((n + 8, n), f32)
    hop_parts = SDS((hops * n, 2 * n), bf16)
    diag_parts = SDS((diags * n, 2 * n), bf16)
    out = SDS((diags + hops, n, n), f32)
    channel = 20 * 8 * 2 * n**3

    (own,) = call(
        first_message,
        (sector_sizes, x0),
        [SMEM, HBM],
        [message],
        scratch=[pltpu.VMEM((n, n), f32), pltpu.SemaphoreType.DMA],
        limit=32,
        name="first_message",
    )
    operators = (dl, hl, dr, hr)
    products = [hop_parts, hop_parts, diag_parts, diag_parts, block]
    arrivals = pltpu.SemaphoreType.DMA((2, PARTS + 1))
    rooms = [pltpu.VMEM(out.shape, f32), pltpu.VMEM(out.shape, f32), arrivals]
    *odd_ops, b = call(
        odd_adjoint,
        (own, *operators),
        [VMEM] + [HBM] * 4,
        products,
        scratch=rooms,
        flops=channel * hops,
        limit=32,
        name="odd_adjoint",
    )
    below0 = lax.ppermute(lax.optimization_barrier((own, b))[0], "blk", up)
    *even_ops, b, d = call(
        even_adjoint,
        (b, own, *operators),
        [VMEM] * 2 + [HBM] * 4,
        [*products, block],
        scratch=rooms,
        flops=channel * hops,
        limit=32,
        name="even_adjoint",
    )
    got_b = lax.ppermute(b, "blk", down)
    ops = (*odd_ops, *even_ops)
    m0, m1 = call(
        odd_gather,
        (below0, *operators),
        [VMEM] + [HBM] * 4,
        [out, out],
        out_specs=[ANY] * 2,
        scratch=[arrivals],
        limit=32,
        name="odd_gather",
    )
    below0 = lax.optimization_barrier((below0, m0))[0]
    (a,) = call(
        by_parity(first_apply),
        (*ops, own, below0, d),
        [VMEM] * 11,
        [block],
        flops=channel * (hops + diags),
        name="apply0",
    )
    for k in range(1, ITERS):
        got_a = lax.ppermute(a, "blk", up)
        if k == 1:
            m0, m1 = call(
                even_gather,
                (lax.optimization_barrier((got_b, a))[0], *operators, m0, m1),
                [VMEM] + [HBM] * 4 + [ANY] * 2,
                [out, out],
                out_specs=[ANY] * 2,
                scratch=[arrivals],
                limit=32,
                aliases={5: 0, 6: 1},
                name="even_gather",
            )
            got_b = lax.optimization_barrier((got_b, m0))[0]
        last_b = b
        v, b, d = call(
            by_parity(adjoint),
            (*ops, own, a, got_b),
            [VMEM] * 11,
            [block, block, block],
            flops=channel * hops,
            name=f"adjoint{k}",
        )
        got_b = lax.ppermute(b, "blk", down)
        if k == ITERS - 1:
            x1 = lax.ppermute(lax.optimization_barrier((m1, b))[0], "seg", across)
            x0 = lax.ppermute(lax.optimization_barrier((m0, b))[0], "seg", chip)
        (a,) = call(
            by_parity(functools.partial(later_apply, k == ITERS - 1)),
            (*ops, own, below0, v, d, got_a, last_b),
            [VMEM] * 14,
            [block],
            flops=channel * (hops + diags),
            name=f"apply{k}",
        )
    sums_block = SDS((blocks, n), f32)
    v4, sums = call(finish, (ranks, own, v, a, got_b), [SMEM] + [VMEM] * 4, [message, sums_block], name="finish")
    members = [(i + blocks // 2 + blocks // 16) % blocks for i in range(blocks)]
    sums = lax.all_to_all(sums, "blk", 0, 0, tiled=True, axis_index_groups=[members])
    state, kept = call(normalise, (v4, sums), [VMEM] * 2, [block, block], name="normalise")
    kept1 = lax.ppermute(kept, "seg", across)
    kept0 = lax.ppermute(kept, "seg", chip)
    all_parts = SDS(((diags + hops) * n, 2 * n), bf16)
    p0, p1, energy = call(
        parts,
        (x0, x1, sums),
        [VMEM] * 3,
        [all_parts, all_parts, SDS((1,), f32)],
        out_specs=[VMEM, VMEM, SMEM],
        flops=channel * hops,
        name="parts",
    )
    state, left, right = call(
        extend,
        (kept1, kept0, p0, p1, state),
        [VMEM] * 5,
        [block, out, out],
        out_specs=[ANY] * 3,
        scratch=[
            pltpu.VMEM(out.shape, f32),
            pltpu.VMEM(out.shape, f32),
            pltpu.SemaphoreType.DMA((1 + 2 * CHUNKS,)),
        ],
        flops=2 * channel * (hops + diags),
        name="extend",
    )
    return state[None, None], left[None, None], right[None, None], energy


def solution(mesh):
    wide = P("seg", "blk", None, None, None)
    return jax.shard_map(
        shards,
        mesh=mesh,
        in_specs=(P("seg", "blk", None, None), wide, wide, wide, wide, P("seg", "blk"), P("seg", "blk")),
        out_specs=(P("seg", "blk", None, None), wide, wide, P("seg")),
        check_vma=False,
    )
```

```python
import functools
import math

import jax
import jax.numpy as jnp
from jax import lax
from jax.experimental import pallas as pl
from jax.experimental.pallas import tpu as pltpu
from jax.sharding import PartitionSpec as P

ITERS = 4
SHIFT = 20.0
BOND = 6144.0
PARTS = 4
CHUNKS = 3
f32 = jnp.float32
bf16 = jnp.bfloat16
VMEM = pl.BlockSpec(memory_space=pltpu.VMEM)
SMEM = pl.BlockSpec(memory_space=pltpu.SMEM)
HBM = pl.BlockSpec(memory_space=pltpu.HBM)
ANY = pl.BlockSpec(memory_space=pl.ANY)
SDS = jax.ShapeDtypeStruct


def dot(a, b):
    return jnp.dot(a, b, preferred_element_type=f32)


def split(x):
    high = x.astype(bf16)
    return high, (x - high.astype(f32)).astype(bf16)


def weight(x):
    high, low = split(x)
    row = jnp.concatenate([high, low], 1)
    return jnp.concatenate([row, row], 0)


def folded(t):
    n = t.shape[1] // 2
    return t[:, :n] + t[:, n:]


def sandwich(p_ref, q_ref, x):
    n = x.shape[0]
    w = weight(x)
    total = None
    for pair in range(p_ref.shape[0] // (2 * n)):
        rows = pl.ds(pair * 2 * n, 2 * n)
        t = folded(dot(p_ref[rows, :], w))
        high, low = split(t)
        lhs = jnp.concatenate(
            [
                jnp.concatenate([high[:n], high[n:]], 1),
                jnp.concatenate([low[:n], low[n:]], 1),
            ],
            0,
        )
        term = dot(lhs, q_ref[rows, :])
        total = term if total is None else total + term
    total = folded(total)
    return total[:n] + total[n:]


def square_mask(size):
    n = size.shape[1]
    size = jnp.broadcast_to(size, (n, n))
    rows = lax.broadcasted_iota(jnp.int32, (n, n), 0).astype(f32)
    cols = lax.broadcasted_iota(jnp.int32, (n, n), 1).astype(f32)
    return (rows < size) & (cols < size)


def where(mask, x):
    return jnp.where(mask, x, 0.0)


def put_parts(out_ref, h, n, x):
    high, low = split(x)
    out_ref[pl.ds(h * n, n), :n] = high
    out_ref[pl.ds(h * n, n), n:] = low


def odd(axis):
    return lax.rem(lax.axis_index(axis), 2) == 1


def load(size_ref, x_ref, dl_ref, hl_ref, dr_ref, hr_ref, own_ref, m0_ref, m1_ref, x, sems):
    n = x.shape[0]
    diags, hops = dl_ref.shape[0], hl_ref.shape[0]
    first = pltpu.make_async_copy(x_ref, x, sems.at[0])
    first.start()
    part = hops // PARTS
    left, right = (dl_ref, hl_ref), (dr_ref, hr_ref)

    def loads(sides):
        copies = []
        for side, ((diag, hop), out) in enumerate(zip(sides, (m0_ref, m1_ref))):
            sem = 1 + side * (1 + PARTS)
            copies.append(pltpu.make_async_copy(diag, out.at[pl.ds(0, diags)], sems.at[sem]))
            for i in range(PARTS):
                source, target = pl.ds(i * part, part), pl.ds(diags + i * part, part)
                copies.append(pltpu.make_async_copy(hop.at[source], out.at[target], sems.at[sem + 1 + i]))
        return copies

    segment = odd("seg")

    @pl.when(segment)
    def _():
        for copy in loads((right, left)):
            copy.start()

    @pl.when(jnp.logical_not(segment))
    def _():
        for copy in loads((left, right)):
            copy.start()

    first.wait()
    live = jnp.full((1, n), size_ref[0, 0].astype(f32), f32)
    own_ref[:n, :] = where(square_mask(live), x[...])
    own_ref[n:, :] = jnp.broadcast_to(live, (8, n))
    for copy in loads((left, right)):
        copy.wait()


def first_product(own_ref, m0_ref, m1_ref, lt_ref, rc_ref, dlt_ref, drc_ref, b_ref):
    n = own_ref.shape[1]
    diags = dlt_ref.shape[0] // n
    segment = odd("seg")
    for c in range(m0_ref.shape[0]):
        x, y = m0_ref[c], m1_ref[c]
        k = c if c < diags else c - diags
        put_parts(dlt_ref if c < diags else lt_ref, k, n, jnp.where(segment, y, x).T)
        put_parts(drc_ref if c < diags else rc_ref, k, n, jnp.where(segment, x, y))
    b_ref[...] = sandwich(lt_ref, rc_ref, own_ref[:n, :])


def odd_adjoint(*refs):
    pl.when(odd("blk"))(lambda: first_product(*refs))


def even_adjoint(own_ref, m0_ref, m1_ref, done_ref, lt_ref, rc_ref, dlt_ref, drc_ref, b_ref):
    @pl.when(odd("blk"))
    def _():
        b_ref[...] = done_ref[...]

    @pl.when(jnp.logical_not(odd("blk")))
    def _():
        first_product(own_ref, m0_ref, m1_ref, lt_ref, rc_ref, dlt_ref, drc_ref, b_ref)


def by_parity(kernel, count):
    def chosen(*refs):
        odd_ops, even_ops, rest = refs[:count], refs[count : 2 * count], refs[2 * count :]
        pl.when(odd("blk"))(lambda: kernel(*odd_ops, *rest))
        pl.when(jnp.logical_not(odd("blk")))(lambda: kernel(*even_ops, *rest))

    return chosen


def adjoint(lt_ref, rc_ref, own_ref, a_ref, got_b_ref, v_ref, b_ref):
    n = own_ref.shape[1]
    v = a_ref[...] - where(square_mask(own_ref[n : n + 1, :]), got_b_ref[...])
    v_ref[...] = v
    b_ref[...] = sandwich(lt_ref, rc_ref, v)


def own_part(own_ref, v, below, lt_ref, rc_ref, dlt_ref, drc_ref):
    n = own_ref.shape[1]
    hop = sandwich(rc_ref, lt_ref, below.T)
    diag = sandwich(drc_ref, dlt_ref, v.T)
    return where(square_mask(own_ref[n : n + 1, :]), (hop + diag).T)


def first_apply(lt_ref, rc_ref, dlt_ref, drc_ref, own_ref, below_ref, a_ref):
    n = own_ref.shape[1]
    v = own_ref[:n, :]
    a_ref[...] = SHIFT * v - own_part(own_ref, v, below_ref[:n, :], lt_ref, rc_ref, dlt_ref, drc_ref)


def later_apply(last, lt_ref, rc_ref, dlt_ref, drc_ref, own_ref, below_ref, v_ref, got_a_ref, b_ref, a_ref):
    n = own_ref.shape[1]
    below = where(square_mask(below_ref[n : n + 1, :]), got_a_ref[...] - b_ref[...])
    v = v_ref[...]
    part = own_part(own_ref, v, below, lt_ref, rc_ref, dlt_ref, drc_ref)
    a_ref[...] = part if last else SHIFT * v - part


def total_of(x):
    return jnp.sum(jnp.sum(x, axis=0, keepdims=True), axis=1, keepdims=True)


def finish(rank_ref, own_ref, v_ref, part_ref, got_b_ref, v4_ref, sums_ref):
    n = own_ref.shape[1]
    v = v_ref[...]
    applied = part_ref[...] + where(square_mask(own_ref[n : n + 1, :]), got_b_ref[...])
    v4 = SHIFT * v - applied
    v4_ref[:n, :] = v4
    kept_cols = jnp.minimum(jnp.full((1, n), rank_ref[0, 0].astype(f32), f32), own_ref[n : n + 1, :])
    v4_ref[n:, :] = jnp.broadcast_to(kept_cols, (8, n))
    lane = lax.broadcasted_iota(jnp.int32, (1, n), 1)
    row = jnp.where(lane == 0, total_of(v4 * v4), 0.0)
    row = jnp.where(lane == 1, total_of(v * applied), row)
    row = jnp.where(lane == 2, total_of(v * v), row)
    sums_ref[...] = jnp.broadcast_to(row, sums_ref.shape)


def lane_of(row, j):
    lane = lax.broadcasted_iota(jnp.int32, row.shape, 1)
    return jnp.sum(jnp.where(lane == j, row, 0.0), axis=1, keepdims=True)


def normalise(v4_ref, sums_ref, state_ref, kept_ref):
    n = v4_ref.shape[1]
    total = jnp.sum(sums_ref[...], axis=0, keepdims=True)
    state = v4_ref[:n, :] * jnp.sqrt(BOND * n / lane_of(total, 0))
    state_ref[...] = state
    cols = lax.broadcasted_iota(jnp.int32, (n, n), 1).astype(f32)
    kept_ref[...] = where(cols < jnp.broadcast_to(v4_ref[n : n + 1, :], (n, n)), state)


def parts(x1_ref, x0_ref, sums_ref, pl_ref, pr_ref, energy_ref):
    n = x0_ref.shape[1]
    segment = odd("seg")
    for c in range(x0_ref.shape[0]):
        x, y = x0_ref[c], x1_ref[c]
        put_parts(pl_ref, c, n, jnp.where(segment, x, y).T)
        put_parts(pr_ref, c, n, jnp.where(segment, y, x))
    total = jnp.sum(sums_ref[...], axis=0, keepdims=True)
    energy_ref[0] = jnp.sum(lane_of(total, 1) / lane_of(total, 2))


def extend(kept1_ref, kept0_ref, pl_ref, pr_ref, state_ref, new_ref, left_ref, right_ref, lo, ro, sems):
    n = kept0_ref.shape[0]
    step = lo.shape[0] // CHUNKS
    copies = [pltpu.make_async_copy(state_ref, new_ref, sems.at[0])]
    copies[0].start()
    segment = odd("seg")
    x, y = kept0_ref[...], kept1_ref[...]
    sides = (
        (pl_ref, weight(jnp.where(segment, x, y)), lo, left_ref),
        (pr_ref, weight(jnp.where(segment, y, x).T), ro, right_ref),
    )
    for i in range(CHUNKS):
        at = pl.ds(i * step, step)
        for side, (p_ref, w, out, target) in enumerate(sides):
            for c in range(i * step, (i + 1) * step, 2):
                half = folded(dot(p_ref[pl.ds(c * n, 2 * n), :], w))
                flip = jnp.concatenate([half[:n].T, half[n:].T], 0)
                z = folded(dot(jnp.concatenate(split(flip), 1), w)) * (1.0 / math.sqrt(n))
                out[c] = z[:n]
                out[c + 1] = z[n:]
            copies.append(pltpu.make_async_copy(out.at[at], target.at[at], sems.at[1 + 2 * i + side]))
            copies[-1].start()
    for copy in copies:
        copy.wait()


def call(kernel, args, specs, outs, out_specs=None, scratch=(), flops=0, limit=16, name=None):
    moved = sum(math.prod(a.shape) * a.dtype.itemsize for a in (*args, *outs))
    args = [pltpu.with_memory_space_constraint(a, pltpu.HBM) if spec is HBM else a for a, spec in zip(args, specs)]
    return pl.pallas_call(
        kernel,
        in_specs=specs,
        out_specs=out_specs or [VMEM] * len(outs),
        out_shape=outs,
        scratch_shapes=list(scratch),
        compiler_params=pltpu.CompilerParams(vmem_limit_bytes=limit << 20),
        cost_estimate=pl.CostEstimate(flops=flops, bytes_accessed=moved, transcendentals=0),
        name=name,
    )(*args)


def shards(two_site, diag_left, diag_right, hop_left, hop_right, sector_sizes, ranks):
    n = two_site.shape[2]
    x0 = two_site[0, 0]
    dl, dr, hl, hr = diag_left[0, 0], diag_right[0, 0], hop_left[0, 0], hop_right[0, 0]
    hops, diags = hl.shape[0], dl.shape[0]
    blocks, segs = lax.axis_size("blk"), lax.axis_size("seg")
    up = [(i, i + 1) for i in range(blocks - 1)]
    down = [(i + 1, i) for i in range(blocks - 1)]
    chip = [(i, i ^ 1) for i in range(segs)]
    across = [(i, i + 1) for i in range(1, segs - 1, 2)]
    across += [(target, source) for source, target in across]
    block = SDS((n, n), f32)
    message = SDS((n + 8, n), f32)
    hop_parts = SDS((hops * n, 2 * n), bf16)
    diag_parts = SDS((diags * n, 2 * n), bf16)
    out = SDS((diags + hops, n, n), f32)
    channel = 20 * 8 * 2 * n**3

    own, m0, m1 = call(
        load,
        (sector_sizes, x0, dl, hl, dr, hr),
        [SMEM] + [HBM] * 5,
        [message, out, out],
        scratch=[
            pltpu.VMEM((n, n), f32),
            pltpu.SemaphoreType.DMA((3 + 2 * PARTS,)),
        ],
        limit=32,
        name="load",
    )
    products = [hop_parts, hop_parts, diag_parts, diag_parts, block]
    *odd_ops, b = call(odd_adjoint, (own, m0, m1), [VMEM] * 3, products, flops=channel * hops, name="odd_adjoint")
    below0 = lax.ppermute(lax.optimization_barrier((own, b))[0], "blk", up)
    *even_ops, b = call(
        even_adjoint, (own, m0, m1, b), [VMEM] * 4, products, flops=channel * hops, name="even_adjoint"
    )
    got_b = lax.ppermute(b, "blk", down)
    ops = (*odd_ops, *even_ops)
    hop_ops = (*odd_ops[:2], *even_ops[:2])
    (a,) = call(
        by_parity(first_apply, 4),
        (*ops, own, below0),
        [VMEM] * 10,
        [block],
        flops=channel * (hops + diags),
        name="apply0",
    )
    for k in range(1, ITERS):
        got_a = lax.ppermute(a, "blk", up)
        last_b = b
        v, b = call(
            by_parity(adjoint, 2),
            (*hop_ops, own, a, got_b),
            [VMEM] * 7,
            [block, block],
            flops=channel * hops,
            name=f"adjoint{k}",
        )
        got_b = lax.ppermute(b, "blk", down)
        if k == ITERS - 1:
            x1 = lax.ppermute(lax.optimization_barrier((m1, b))[0], "seg", across)
            x0 = lax.ppermute(lax.optimization_barrier((m0, b))[0], "seg", chip)
        (a,) = call(
            by_parity(functools.partial(later_apply, k == ITERS - 1), 4),
            (*ops, own, below0, v, got_a, last_b),
            [VMEM] * 13,
            [block],
            flops=channel * (hops + diags),
            name=f"apply{k}",
        )
    sums_block = SDS((blocks, n), f32)
    v4, sums = call(finish, (ranks, own, v, a, got_b), [SMEM] + [VMEM] * 4, [message, sums_block], name="finish")
    members = [(i + blocks // 2 + blocks // 16) % blocks for i in range(blocks)]
    sums = lax.all_to_all(sums, "blk", 0, 0, tiled=True, axis_index_groups=[members])
    state, kept = call(normalise, (v4, sums), [VMEM] * 2, [block, block], name="normalise")
    kept1 = lax.ppermute(kept, "seg", across)
    kept0 = lax.ppermute(kept, "seg", chip)
    all_parts = SDS(((diags + hops) * n, 2 * n), bf16)
    p0, p1, energy = call(
        parts,
        (x1, x0, sums),
        [VMEM] * 3,
        [all_parts, all_parts, SDS((1,), f32)],
        out_specs=[VMEM, VMEM, SMEM],
        flops=channel * hops,
        name="parts",
    )
    state, left, right = call(
        extend,
        (kept1, kept0, p0, p1, state),
        [VMEM] * 5,
        [block, out, out],
        out_specs=[ANY] * 3,
        scratch=[
            pltpu.VMEM(out.shape, f32),
            pltpu.VMEM(out.shape, f32),
            pltpu.SemaphoreType.DMA((1 + 2 * CHUNKS,)),
        ],
        flops=2 * channel * (hops + diags),
        name="extend",
    )
    return state[None, None], left[None, None], right[None, None], energy


def solution(mesh):
    wide = P("seg", "blk", None, None, None)
    return jax.shard_map(
        shards,
        mesh=mesh,
        in_specs=(P("seg", "blk", None, None), wide, wide, wide, wide, P("seg", "blk"), P("seg", "blk")),
        out_specs=(P("seg", "blk", None, None), wide, wide, P("seg")),
        check_vma=False,
    )
```
